128 devices in a mesh: strike: 32 (over y, x, core), depth: 4 (over z).
Axes of the slice: x: 4, y: 4, z: 4, core: 2. Of those that a mesh axis runs over, the one named last changes fastest.
Arguments:
- forward_field: float32 [3, 512, 64, 512], P(None, 'strike', 'depth'), may hold values from -6 to 6
- adjoint_start: float32 [3, 512, 64, 512], P(None, 'strike', 'depth'), may hold values from -6 to 6
- modulus: float32 [512, 64, 512], P('strike', 'depth'), may hold values from 0.5 to 5
- misfit: float32 [3, 32768], P(None, ('strike', 'depth')), may hold values from -24 to 24
- row_owner: int32 [32768, 1], P(('strike', 'depth')), may hold values from 0 to 127; in each aligned block of 256 rows (0 to 255, 256 to 511, ...) at most 8 rows name the same one
- row_cell: int32 [32768], P(('strike', 'depth')), may hold values from 0 to 255
Outputs:
- adjoint: float32 [3, 512, 64, 512], P(None, 'strike', 'depth')
- gradient: float32 [512, 64, 512], P('strike', 'depth')
The draws below stay inside these ranges and needn't reach their ends.
Inputs may be any that keep to these rules, and one draw needn't show every extreme that they name: `row_owner`: in the rows of one device no owner is named more than 8 times, a bound that some block reaches.
All inputs are finite; a program needn't handle non-finite values.
Results may differ from the reference program's by a relative error of at most 0.0003.
Values sent between devices are 32-bit elements; how exact they have to be, the bound alone decides.
A program may use at most 128 MiB of HBM per device.

```python
import math
import jax
import jax.numpy as jnp
import numpy as np
from jax import lax

CS = 16
CD = 16
NN = 512
ITERS = 3
ROWS_DEV = 256
CAP = 8
NS = 512
ND = 64
ROWS = 32768
N_STRIKE = 32
N_DEPTH = 4


def set_ends(values, rng, least, high):
    longest = values.shape.index(max(values.shape))
    spots = []
    for shift in (0, 1):
        where = [jax.random.randint(jax.random.fold_in(rng, axis), (), 0, length) for axis, length in enumerate(values.shape)]
        where[longest] = (where[longest] + shift) % values.shape[longest]
        spots.append(tuple(where))
    return values.at[spots[0]].set(least).at[spots[1]].set(high)


def shard_levels(rng, dims, split, low, largest):
    def one(position, blocks):
        draws = jax.random.uniform(jax.random.fold_in(jax.random.fold_in(rng, 6), position), (blocks,), jnp.float32, low / len(split), largest / len(split))
        return jnp.repeat(jnp.exp(draws), dims[position] // blocks).reshape((-1,) + (1,) * (len(dims) - position - 1))

    level = one(*split[0])
    for cut in split[1:]:
        level = level * one(*cut)
    return level


def assign_block(own_key, own, number, rows, amount, top, limit, slope):
    ranking = jax.random.permutation(own_key, amount)
    crowded, usual = shares(amount, rows * top, limit, slope, True), shares(amount, rows * top, limit, slope, False)
    places = jnp.arange(amount)

    def named(tallies, offset_by):
        used = int((tallies > 0).sum())
        fixed = max(1, used // 4)
        moved = fixed + (places - fixed + offset_by * (used - fixed)) % max(1, amount - fixed)
        return jnp.zeros((amount,), jnp.int32).at[ranking[jnp.where(places < fixed, places, moved)]].set(jnp.asarray(tallies, jnp.int32))

    tallies = jnp.where(number % 4 == 0, named(crowded, number // 4), named(usual, number - number // 4 - 1))
    mixed = jax.random.permutation(jax.random.fold_in(own, 3), amount)
    giver, taker = mixed[0:amount // 2 * 2:2], mixed[1:amount // 2 * 2:2]
    margin = jnp.minimum(tallies[giver] - 1, limit - tallies[taker]) // 2
    margin = jnp.where((giver == ranking[0]) | (taker == ranking[0]) | (tallies[taker] == 0), 0, jnp.maximum(margin, 0))
    moved = jax.random.randint(jax.random.fold_in(own, 4), (amount // 2,), 0, 1 << 20) % (margin + 1)
    tallies = tallies.at[giver].add(-moved).at[taker].add(moved)
    labels = jnp.searchsorted(jnp.cumsum(tallies), jnp.arange(rows * top), side="right").astype(jnp.int32)
    table = labels.reshape(top, rows).T
    table = table[jax.random.permutation(jax.random.fold_in(own, 1), rows)]
    offset_by = jax.random.randint(jax.random.fold_in(own, 2), (rows, 1), 0, top)
    return jnp.take_along_axis(table, (jnp.arange(top)[None, :] + offset_by) % top, axis=1)


def shares(number_of, total, bound, skew, full):
    portions = [(1 << 20) // math.isqrt(grade ** skew) + 1 for grade in range(1, number_of + 1)]
    largest = bound if full else min(bound, max(-(-total // number_of), total * portions[0] // sum(portions)))
    least = 1 if total - largest >= number_of - 1 else 0
    holding, rest = [largest] + [least] * (number_of - 1), total - largest - least * (number_of - 1)
    while rest > 0:
        movable = [i for i in range(1, number_of) if holding[i] < largest] or [i for i in range(1, number_of) if holding[i] < bound]
        whole, remaining = sum([portions[i] for i in movable]), rest
        for i in movable:
            extra = min(bound - holding[i], max(1, remaining * portions[i] // whole), rest)
            holding[i] = holding[i] + extra
            rest = rest - extra
    return np.array(holding)


def scatter_about(stream_key, dims, width, most, cuts=(), dtype=jnp.bfloat16):
    values = jax.random.normal(stream_key, dims, jnp.float32) * width
    if len(cuts) > 0:
        values = shard_levels(stream_key, dims, cuts, -0.22, 0.18) * values
    return jnp.clip(values, min=-most, max=most).astype(dtype)


def setup_inputs(seed: int = 0) -> dict:
    arg_keys = jax.random.split(jax.random.key(seed), 7)
    forward_field = scatter_about(arg_keys[0], (3, NS, ND, NN), 1.0, 6.0, ((1, 32), (2, 4)), jnp.float32)
    adjoint_start = jnp.clip(jax.random.uniform(arg_keys[1], (3, NS, ND, NN), jnp.float32, -6.0, 6.0) * shard_levels(arg_keys[1], (3, NS, ND, NN), ((1, 32), (2, 4)), -0.4, 0.0), -6.0, 6.0)
    modulus = jnp.clip(jnp.exp(math.log(5.0) - 2.3025851 * jax.random.uniform(arg_keys[2], (NS, ND, NN), jnp.float32) ** shard_levels(arg_keys[2], (NS, ND, NN), ((0, 32), (1, 4)), -0.2, 0.2)), 0.5, 5.0)
    misfit = scatter_about(arg_keys[3], (3, ROWS), 4.0, 24.0, ((1, 128),), jnp.float32)
    row_owner_keys = jax.random.split(jax.random.fold_in(arg_keys[4], 1), ROWS // ROWS_DEV)
    row_owner_turns = jax.random.permutation(jax.random.fold_in(arg_keys[4], 3), ROWS // ROWS_DEV)
    row_owner = jax.vmap(lambda own, number: assign_block(jax.random.fold_in(arg_keys[4], 2), own, number, ROWS_DEV, N_STRIKE * N_DEPTH, 1, CAP, 2))(row_owner_keys, row_owner_turns).reshape((ROWS, 1))
    row_cell = set_ends(jax.random.randint(arg_keys[5], (ROWS,), 0, CS * CD), jax.random.fold_in(arg_keys[5], 1), 0, (CS * CD) - 1).astype(jnp.int32)
    return dict(forward_field=forward_field, adjoint_start=adjoint_start, modulus=modulus, misfit=misfit, row_owner=row_owner, row_cell=row_cell)


penalty_weight = 4.0


def face_moduli(padded, modulus):
    uppers = [padded[2:, 1:-1, 1:-1], padded[1:-1, 2:, 1:-1], padded[1:-1, 1:-1, 2:]]
    lowers = [padded[:-2, 1:-1, 1:-1], padded[1:-1, :-2, 1:-1], padded[1:-1, 1:-1, :-2]]
    upper_coef = [0.5 * (modulus + beside) for beside in uppers]
    lower_coef = [0.5 * (modulus + beside) for beside in lowers]
    fault_mask = (lax.broadcasted_iota(jnp.int32, modulus.shape, 2) == 0).astype(jnp.float32)
    fault_term = penalty_weight * modulus * fault_mask
    diagonal = fault_term
    for number in range(3):
        diagonal = diagonal + upper_coef[number] + lower_coef[number]
    return upper_coef, lower_coef, fault_term, diagonal


def apply_operator(padded, field, upper_coef, lower_coef, fault_term):
    uppers = [padded[:, 2:, 1:-1, 1:-1], padded[:, 1:-1, 2:, 1:-1], padded[:, 1:-1, 1:-1, 2:]]
    lowers = [padded[:, :-2, 1:-1, 1:-1], padded[:, 1:-1, :-2, 1:-1], padded[:, 1:-1, 1:-1, :-2]]
    result = fault_term * field
    for number in range(3):
        result = result + upper_coef[number] * (field - uppers[number]) + lower_coef[number] * (field - lowers[number])
    return result


def strain_product(padded):
    diffs = [padded[:, 2:, 1:-1, 1:-1] - padded[:, :-2, 1:-1, 1:-1],
             padded[:, 1:-1, 2:, 1:-1] - padded[:, 1:-1, :-2, 1:-1],
             padded[:, 1:-1, 1:-1, 2:] - padded[:, 1:-1, 1:-1, :-2]]
    result = jnp.zeros(padded.shape[1:], jnp.float32)[:-2, :-2, :-2]
    for number in range(3):
        halved = 0.5 * diffs[number]
        result = result - jnp.sum(halved[:3] * halved[3:], axis=0)
    return result


def pad_field(field):
    return jnp.pad(field, ((0, 0), (1, 1), (1, 1), (1, 1)))


def reference(forward_field, adjoint_start, modulus, misfit, row_owner, row_cell):
    owner = row_owner[:, 0]
    strike_idx = (owner // N_DEPTH) * CS + row_cell // CD
    depth_idx = (owner % N_DEPTH) * CD + row_cell % CD
    plane = jnp.zeros((3, NS, ND), jnp.float32).at[:, strike_idx, depth_idx].add(misfit)
    source = jnp.zeros((3, NS, ND, NN), jnp.float32).at[:, :, :, 0].set(plane)
    upper_coef, lower_coef, fault_term, diagonal = face_moduli(jnp.pad(modulus, 1), modulus)
    adjoint = adjoint_start
    remain = source - apply_operator(pad_field(adjoint_start), adjoint_start, upper_coef, lower_coef, fault_term)
    scaled = remain / diagonal
    search = scaled
    energy = jnp.sum(remain * scaled)
    for turn_index in range(ITERS):
        applied = apply_operator(pad_field(search), search, upper_coef, lower_coef, fault_term)
        step_len = energy / jnp.sum(search * applied)
        adjoint = adjoint + step_len * search
        remain = remain - step_len * applied
        scaled = remain / diagonal
        fresh = jnp.sum(remain * scaled)
        search = scaled + (fresh / energy) * search
        energy = fresh
    gradient = strain_product(pad_field(jnp.concatenate([forward_field, adjoint], 0)))
    return adjoint, gradient
```

```python
import jax
import jax.numpy as jnp
from jax import lax
from jax.experimental import pallas as pl
from jax.experimental.pallas import tpu as pltpu
from jax.sharding import PartitionSpec as P

MESH = pl.DeviceIdType.MESH
C, S, D, N = 3, 16, 16, 512
NS_DEV, ND_DEV = 32, 4
CAP = 8
PENALTY = 4.0
f32 = jnp.float32
FM, FX, FF, F0, F1, F2 = range(6)


def halves(v):
    hi = v.astype(jnp.bfloat16)
    rest = v - hi.astype(f32)
    mid = rest.astype(jnp.bfloat16)
    lo = (rest - mid.astype(f32)).astype(jnp.bfloat16)
    return hi, mid, lo


def lane_low(v):
    return pltpu.roll(v, 1, 1)


def lane_high(v):
    return pltpu.roll(v, N - 1, 1)


def rows_low(v, halo):
    row = lax.broadcasted_iota(jnp.int32, v.shape, 0)
    return jnp.where(row == 0, jnp.broadcast_to(halo, v.shape), pltpu.roll(v, 1, 0))


def rows_high(v, halo):
    row = lax.broadcasted_iota(jnp.int32, v.shape, 0)
    return jnp.where(row == D - 1, jnp.broadcast_to(halo, v.shape), pltpu.roll(v, D - 1, 0))


def kernel(f_hbm, x_hbm, m_hbm, mis_ref, own_ref, cell_ref, adj_ref, grad_ref,
           mb, xb, fb, ub, hm, hx, hf, hu, sm, sx, sf, su, coef, diag, inv,
           msg1, got1, msg2, got2, red, got3, got4,
           load_sem, ssem, rsem, s1, r1, s2, r2, s3, r3, s4, r4):
    si, di = lax.axis_index("strike"), lax.axis_index("depth")
    core, chip = lax.rem(si, 2), si // 2
    near = core * 4 + di

    loads = [
        pltpu.make_async_copy(m_hbm, mb.at[pl.ds(1, S)], load_sem.at[0]),
        pltpu.make_async_copy(x_hbm, xb.at[:, pl.ds(1, S)], load_sem.at[1]),
        pltpu.make_async_copy(f_hbm, fb.at[:, pl.ds(1, S)], load_sem.at[2]),
    ]
    for load in loads:
        load.start()

    def near_dev(k):
        t = lax.rem(near + k, 8)
        return (chip * 2 + t // 4, lax.rem(t, 4)), t

    def far_dev(k):
        t = lax.rem(chip + k, 16)
        return (t * 2 + core, di), t

    strike_up, strike_dn = lax.rem(si + 1, NS_DEV), lax.rem(si + NS_DEV - 1, NS_DEV)
    barrier = pltpu.get_barrier_semaphore()
    for t in (strike_up, strike_dn):
        pl.semaphore_signal(barrier, inc=1, device_id=(t, di), device_id_type=MESH)
    for k in range(1, 8):
        pl.semaphore_signal(barrier, inc=1, device_id=near_dev(k)[0], device_id_type=MESH)
    for k in range(1, 16):
        pl.semaphore_signal(barrier, inc=1, device_id=far_dev(k)[0], device_id_type=MESH)

    @pl.when(si == 0)
    def _():
        mb[0] = jnp.zeros((D, N), f32)
        for buf in (xb, fb):
            buf[:, 0] = jnp.zeros((C, D, N), f32)
        ub[:, :, 0] = jnp.zeros((3, C, D, N), f32)

    @pl.when(si == NS_DEV - 1)
    def _():
        mb[S + 1] = jnp.zeros((D, N), f32)
        for buf in (xb, fb):
            buf[:, S + 1] = jnp.zeros((C, D, N), f32)
        ub[:, :, S + 1] = jnp.zeros((3, C, D, N), f32)

    for edge, side in ((0, 0), (ND_DEV - 1, 1)):
        @pl.when(di == edge)
        def _(side=side):
            hm[side] = jnp.zeros((S, N), f32)
            hx[side] = jnp.zeros((C, S, N), f32)
            hf[side] = jnp.zeros((C, S, N), f32)
            hu[:, side] = jnp.zeros((3, C, S, N), f32)

    owner, cell = own_ref[...], cell_ref[...]
    rows = owner.shape[1]
    same = (lax.broadcasted_iota(jnp.int32, (128, rows), 0) == owner).astype(f32)
    before = (lax.broadcasted_iota(jnp.int32, (rows, rows), 0)
              < lax.broadcasted_iota(jnp.int32, (rows, rows), 1)).astype(f32).astype(jnp.bfloat16)
    count = jnp.dot(same.astype(jnp.bfloat16), before, preferred_element_type=f32)
    rank = jnp.sum(same * count, axis=0, keepdims=True)
    place = owner * CAP + rank.astype(jnp.int32)
    values = jnp.concatenate([mis_ref[...], cell.astype(f32), jnp.zeros((4, rows), f32)], axis=0)
    parts = jnp.concatenate([p.astype(f32) for p in halves(values)], axis=0).astype(jnp.bfloat16)
    slots = 8 * CAP
    for q in range(16):
        hot = (lax.broadcasted_iota(jnp.int32, (slots, rows), 0) + q * slots == place).astype(f32)
        out = lax.dot_general(parts, hot.astype(jnp.bfloat16), (((1,), (1,)), ((), ())),
                              preferred_element_type=f32)
        msg1[q, :, 0:slots] = (out[0:8] + out[8:16] + out[16:24])[0:4]
        msg1[q, :, slots:128] = jnp.zeros((4, 128 - slots), f32)

    def halo_copies(field):
        if field == FM:
            buf, halo, stage = mb, hm, sm
            lane = (lambda i: buf.at[i])
        elif field == FX:
            buf, halo, stage = xb, hx, sx
            lane = (lambda i: buf.at[:, i])
        elif field == FF:
            buf, halo, stage = fb, hf, sf
            lane = (lambda i: buf.at[:, i])
        else:
            k = field - F0
            buf, halo, stage = ub, hu.at[k], su.at[k]
            lane = (lambda i: buf.at[k, :, i])

        def copy(src, dst, way, t):
            return pltpu.make_async_remote_copy(src_ref=src, dst_ref=dst, send_sem=ssem.at[field, way],
                                                recv_sem=rsem.at[field, way], device_id=t, device_id_type=MESH)

        return [
            (di < ND_DEV - 1, di > 0, copy(stage.at[1], halo.at[0], 0, (si, lax.rem(di + 1, ND_DEV)))),
            (di > 0, di < ND_DEV - 1, copy(stage.at[0], halo.at[1], 1, (si, lax.rem(di + ND_DEV - 1, ND_DEV)))),
            (si < NS_DEV - 1, si > 0, copy(lane(S), lane(0), 2, (strike_up, di))),
            (si > 0, si < NS_DEV - 1, copy(lane(1), lane(S + 1), 3, (strike_dn, di))),
        ]

    def send(field):
        for has, _, copy in halo_copies(field):
            pl.when(has)(copy.start)

    def recv(field):
        for _, gets, copy in halo_copies(field):
            pl.when(gets)(copy.wait_recv)

    def sent(field):
        for has, _, copy in halo_copies(field):
            pl.when(has)(copy.wait_send)

    def stage_rows(read, stage):
        for s in range(S):
            v = read(s)
            for c in range(C):
                stage[0, c, s:s + 1] = v[c, 0:1]
                stage[1, c, s:s + 1] = v[c, D - 1:D]

    loads[0].wait()
    for s in range(S):
        sm[0, s:s + 1] = mb[s + 1, 0:1]
        sm[1, s:s + 1] = mb[s + 1, D - 1:D]
    loads[1].wait()
    stage_rows(lambda s: xb[:, s + 1], sx)
    pl.semaphore_wait(barrier, 24)
    send(FM)
    send(FX)

    def far_copy(k):
        (t, idx) = far_dev(k)
        return pltpu.make_async_remote_copy(src_ref=msg1.at[idx], dst_ref=got1.at[chip], send_sem=s1.at[k],
                                            recv_sem=r1.at[k], device_id=t, device_id_type=MESH)

    for k in range(1, 16):
        far_copy(k).start()
    got1[chip] = msg1[chip]
    loads[2].wait()
    stage_rows(lambda s: fb[:, s + 1], sf)
    for k in range(1, 16):
        far_copy(k).wait_recv()

    slot_lane = lax.broadcasted_iota(jnp.int32, (1, 128), 1)
    total = jnp.zeros((3 * 3 * 64, 128), f32)
    for half in range(2):
        offs, picks = [], []
        for q in range(8 * half, 8 * half + 8):
            row = got1[q]
            at = row[3:4].astype(jnp.int32)
            brick = slot_lane // CAP
            at_s = (brick // 4) * S + at // D
            at_d = lax.rem(brick, 4) * D + lax.rem(at, D)
            live = slot_lane < slots
            picks.append((jnp.where(live, at_s, -1), jnp.where(live, at_d, -1), row))
        hot_s = jnp.concatenate([(lax.broadcasted_iota(jnp.int32, (128, 128), 0) == p[0]).astype(f32) for p in picks],
                                axis=1).astype(jnp.bfloat16)
        lines = []
        is_d = [lax.broadcasted_iota(jnp.int32, (64, 128), 0) == p[1] for p in picks]
        vals = [[part.astype(f32) for part in halves(p[2])] for p in picks]
        for c in range(C):
            for part in range(3):
                lines.append(jnp.concatenate(
                    [jnp.where(is_d[j], vals[j][part][c:c + 1], 0.0) for j in range(8)], axis=1))
        left = jnp.concatenate(lines, axis=0).astype(jnp.bfloat16)
        total = total + lax.dot_general(left, hot_s, (((1,), (1,)), ((), ())), preferred_element_type=f32)
    for c in range(C):
        dense = total[(3 * c) * 64:(3 * c + 1) * 64] + total[(3 * c + 1) * 64:(3 * c + 2) * 64] \
            + total[(3 * c + 2) * 64:(3 * c + 3) * 64]
        for t in range(8):
            part = dense[(t % 4) * D:(t % 4 + 1) * D]
            msg2[t, c] = part if t < 4 else pltpu.roll(part, 128 - S, 1)

    def near_copy(src, dst, send_sem, recv_sem, k, t):
        return pltpu.make_async_remote_copy(src_ref=src, dst_ref=dst, send_sem=send_sem.at[k],
                                            recv_sem=recv_sem.at[k], device_id=t, device_id_type=MESH)

    def plane_copy(k):
        t, idx = near_dev(k)
        return near_copy(msg2.at[idx], got2.at[near], s2, r2, k, t)

    for k in range(1, 8):
        plane_copy(k).start()
    got2[near] = msg2[near]

    recv(FM)
    first = lax.broadcasted_iota(jnp.int32, (D, N), 1) == 0
    last = lax.broadcasted_iota(jnp.int32, (D, N), 1) == N - 1

    def coefs(s, _):
        m = mb[s + 1]
        beside = [mb[s], mb[s + 2], rows_low(m, hm[0, pl.ds(s, 1)]), rows_high(m, hm[1, pl.ds(s, 1)]),
                  jnp.where(first, 0.0, lane_low(m)), jnp.where(last, 0.0, lane_high(m))]
        face = [0.5 * (m + b) for b in beside]
        dd = jnp.where(first, PENALTY * m, 0.0)
        for a in face:
            dd = dd + a
        ii = 1.0 / dd
        diag[s] = dd
        inv[s] = ii
        row = lax.broadcasted_iota(jnp.int32, (D, N), 0)
        outside = [(s + si == 0), (s + si == S - 1 + NS_DEV - 1), (row == 0) & (di == 0),
                   (row == D - 1) & (di == ND_DEV - 1), first, last]
        for j in range(6):
            if j < 2:
                coef[j, s] = face[j] * ii
            else:
                coef[j, s] = jnp.where(outside[j], 0.0, face[j] * ii)
        return 0

    lax.fori_loop(0, S, coefs, 0)

    def sweep(read, halo, c, s):
        v = read(c, s + 1)
        out = coef[0, s] * read(c, s) + coef[1, s] * read(c, s + 2)
        out = out + coef[2, s] * rows_low(v, halo[0, c, pl.ds(s, 1)]) + coef[3, s] * rows_high(v, halo[1, c, pl.ds(s, 1)])
        return v, out + coef[4, s] * lane_low(v) + coef[5, s] * lane_high(v)

    recv(FX)

    def start_field(s, _):
        for c in range(C):
            v, w = sweep(lambda c, i: xb[c, i], hx, c, s)
            ub[0, c, s + 1] = w - v
        return 0

    lax.fori_loop(0, S, start_field, 0)
    for k in range(1, 8):
        plane_copy(k).wait_recv()
    lane0 = lax.broadcasted_iota(jnp.int32, (D, 128), 1) == 0
    for c in range(C):
        plane = got2[0, c]
        for j in range(1, 8):
            plane = plane + got2[j, c]
        for s in range(S):
            mine = plane if s == 0 else pltpu.roll(plane, 128 - s, 1)
            ub[0, c, s + 1, :, 0:128] += jnp.where(lane0, mine * inv[s, :, 0:128], 0.0)

    def fold(v):
        w = v[0:8] + v[8:16]
        return w[:, 0:128] + w[:, 128:256] + w[:, 256:384] + w[:, 384:512]

    zero8 = jnp.zeros((8, 128), f32)
    for k in range(3):
        stage_rows(lambda s, k=k: ub[k, :, s + 1], su.at[k])
        send(F0 + k)
        if k == 2:
            send(FF)
        recv(F0 + k)

        def step(s, sums, k=k):
            sums = list(sums)
            dd = diag[s]
            for c in range(C):
                v, w = sweep(lambda c, i: ub[k, c, i], hu.at[k], c, s)
                if k < 2:
                    ub[k + 1, c, s + 1] = w
                du = dd * v
                diff = v - w
                sums[0] = sums[0] + fold(du * v)
                sums[1] = sums[1] + fold(du * diff)
                sums[2] = sums[2] + fold(dd * (w * diff))
                sums[3] = sums[3] + fold(du * w)
            return tuple(sums)

        got = lax.fori_loop(0, S, step, (zero8,) * 4)
        for j in range(4):
            red[0, pl.ds(4 * k + j, 1)] = jnp.sum(got[j], axis=0, keepdims=True)
    red[0, pl.ds(12, 4)] = jnp.zeros((4, 128), f32)

    got3[chip] = red[0]

    def sum_copy(k):
        t, _ = far_dev(k)
        return near_copy(red.at[0], got3.at[chip], s3, r3, k, t)

    for k in range(1, 16):
        sum_copy(k).start()
    for k in range(1, 16):
        sum_copy(k).wait_recv()
    part = got3[0]
    for j in range(1, 16):
        part = part + got3[j]
    red[1] = part
    got4[near] = part

    def last_copy(k):
        t, _ = near_dev(k)
        return near_copy(red.at[1], got4.at[near], s4, r4, k, t)

    for k in range(1, 8):
        last_copy(k).start()
    for k in range(1, 8):
        last_copy(k).wait_recv()
    part = got4[0]
    for j in range(1, 8):
        part = part + got4[j]
    tot = jnp.sum(part, axis=1, keepdims=True)

    def at(i):
        return tot[i:i + 1]

    b0, b1, b2 = at(0), at(3), at(4)
    g0, g1, g2, g3, g4 = at(1), at(2), at(5), at(6), at(9)
    l1, l2 = g1 / g0, g2 / g0
    s11, s12, s22 = g2 - l1 * g1, g3 - l1 * g2, g4 - l2 * g2
    y1, y2 = b1 - l1 * b0, b2 - l2 * b0
    l3 = s12 / s11
    c2 = (y2 - l3 * y1) / (s22 - l3 * s12)
    c1 = (y1 - s12 * c2) / s11
    c0 = (b0 - g1 * c1 - g2 * c2) / g0

    def combine(x, u):
        return x + c0 * u[0] + c1 * u[1] + c2 * u[2]

    recv(FF)
    sent(FX)

    def adjoint_cells(s, _):
        for c in range(C):
            xb[c, s] = combine(xb[c, s], [ub[k, c, s] for k in range(3)])
        return 0

    lax.fori_loop(0, S + 2, adjoint_cells, 0)
    for side in range(2):
        for c in range(C):
            hx[side, c] = combine(hx[side, c], [hu[k, side, c] for k in range(3)])

    def gradient_cells(s, _):
        total = jnp.zeros((D, N), f32)
        for c in range(C):
            a, b = xb[c, s + 1], fb[c, s + 1]
            adj_ref[c, s] = a
            da = xb[c, s + 2] - xb[c, s]
            db = fb[c, s + 2] - fb[c, s]
            total = total + da * db
            da = rows_high(a, hx[1, c, pl.ds(s, 1)]) - rows_low(a, hx[0, c, pl.ds(s, 1)])
            db = rows_high(b, hf[1, c, pl.ds(s, 1)]) - rows_low(b, hf[0, c, pl.ds(s, 1)])
            total = total + da * db
            da = jnp.where(last, 0.0, lane_high(a)) - jnp.where(first, 0.0, lane_low(a))
            db = jnp.where(last, 0.0, lane_high(b)) - jnp.where(first, 0.0, lane_low(b))
            total = total + da * db
        grad_ref[s] = -0.25 * total
        return 0

    lax.fori_loop(0, S, gradient_cells, 0)
    for k in range(1, 16):
        far_copy(k).wait_send()
        sum_copy(k).wait_send()
    for k in range(1, 8):
        plane_copy(k).wait_send()
        last_copy(k).wait_send()
    for field in (FM, FF, F0, F1, F2):
        sent(field)


def on_device(forward_field, adjoint_start, modulus, misfit, row_owner, row_cell):
    rows = row_cell.shape[0]
    vm = pltpu.VMEM
    dma = pltpu.SemaphoreType.DMA
    field = vm((C, S + 2, D, N), f32)
    face = vm((2, C, S, N), f32)
    anywhere, inside = pl.BlockSpec(memory_space=pl.ANY), pl.BlockSpec(memory_space=pltpu.VMEM)
    return pl.pallas_call(
        kernel,
        out_shape=(jax.ShapeDtypeStruct((C, S, D, N), f32), jax.ShapeDtypeStruct((S, D, N), f32)),
        in_specs=[anywhere] * 3 + [inside] * 3,
        out_specs=(inside, inside),
        scratch_shapes=[
            vm((S + 2, D, N), f32), field, field, vm((3, C, S + 2, D, N), f32),
            vm((2, S, N), f32), face, face, vm((3, 2, C, S, N), f32),
            vm((2, S, N), f32), face, face, vm((3, 2, C, S, N), f32),
            vm((6, S, D, N), f32), vm((S, D, N), f32), vm((S, D, N), f32),
            vm((16, 4, 128), f32), vm((16, 4, 128), f32),
            vm((8, C, D, 128), f32), vm((8, C, D, 128), f32),
            vm((2, 16, 128), f32), vm((16, 16, 128), f32), vm((8, 16, 128), f32),
            dma((3,)), dma((6, 4)), dma((6, 4)),
            dma((16,)), dma((16,)), dma((8,)), dma((8,)), dma((16,)), dma((16,)), dma((8,)), dma((8,)),
        ],
        compiler_params=pltpu.CompilerParams(collective_id=0, has_side_effects=True, vmem_limit_bytes=48 << 20),
        name="window",
    )(forward_field, adjoint_start, modulus, misfit, row_owner.reshape(1, rows), row_cell.reshape(1, rows))


def solution(mesh):
    placed = (
        P(None, "strike", "depth", None),
        P(None, "strike", "depth", None),
        P("strike", "depth", None),
        P(None, ("strike", "depth")),
        P(("strike", "depth"), None),
        P(("strike", "depth")),
    )
    return jax.shard_map(
        on_device,
        mesh=mesh,
        in_specs=placed,
        out_specs=(P(None, "strike", "depth", None), P("strike", "depth", None)),
        check_vma=False,
    )
```

```python
import jax
import jax.numpy as jnp
from jax import lax
from jax.experimental import pallas as pl
from jax.experimental.pallas import tpu as pltpu
from jax.sharding import PartitionSpec as P

MESH = pl.DeviceIdType.MESH
C, S, D, N = 3, 16, 16, 512
NS_DEV, ND_DEV = 32, 4
CAP = 8
PENALTY = 4.0
f32, bf16, i32 = jnp.float32, jnp.bfloat16, jnp.int32
UNROLL = 4


def iota(shape, dim):
    return lax.broadcasted_iota(i32, shape, dim)


def thirds(v):
    hi = v.astype(bf16)
    rest = v - hi.astype(f32)
    mid = rest.astype(bf16)
    return hi, mid, (rest - mid.astype(f32)).astype(bf16)


def cols_low(v):
    return pltpu.roll(v, 1, 1)


def cols_high(v):
    return pltpu.roll(v, N - 1, 1)


def rows_low(v, halo):
    row = iota((8, N), 0)
    top, low = pltpu.roll(v[0:8], 1, 0), pltpu.roll(v[8:16], 1, 0)
    return jnp.concatenate([jnp.where(row == 0, jnp.broadcast_to(halo, (8, N)), top), jnp.where(row == 0, top, low)], 0)


def rows_high(v, halo):
    row = iota((8, N), 0)
    top, low = pltpu.roll(v[0:8], 7, 0), pltpu.roll(v[8:16], 7, 0)
    return jnp.concatenate([jnp.where(row == 7, low, top), jnp.where(row == 7, jnp.broadcast_to(halo, (8, N)), low)], 0)


def fold(v):
    w = v[0:8, 128:N] + v[8:16, 128:N]
    return w[:, 0:128] + w[:, 128:256] + w[:, 256:384]


def window(f_hbm, x_hbm, m_hbm, mis_hbm, own_hbm, cell_hbm, xb, ub, gb, cv,
           mb, fb, mf, xf, ff, uf, ms, xs, fs, us, mc, xc, uc, coef, diag, u3, wb, mis, own, cel,
           msg1, got1, msg2, got2, red, got3, got4,
           load_sem, ssem, rsem, cssem, crsem, wssem, wrsem, s1, r1, s2, r2, s3, r3, s4, r4):
    si, di = lax.axis_index("strike"), lax.axis_index("depth")
    core, chip = lax.rem(si, 2), si // 2
    near = core * 4 + di
    up_s, dn_s = lax.rem(si + 1, NS_DEV), lax.rem(si + NS_DEV - 1, NS_DEV)
    up_d, dn_d = lax.rem(di + 1, ND_DEV), lax.rem(di + ND_DEV - 1, ND_DEV)
    not_first_s, not_last_s = si > 0, si < NS_DEV - 1
    not_first_d, not_last_d = di > 0, di < ND_DEV - 1

    loads = [pltpu.make_async_copy(src, dst, load_sem.at[j]) for j, (src, dst) in enumerate((
        (mis_hbm, mis), (own_hbm, own), (cell_hbm, cel), (m_hbm, mb.at[pl.ds(2, S)]),
        (x_hbm, xb.at[:, pl.ds(2, S)]), (f_hbm, fb.at[:, pl.ds(1, S)])))]
    for load in loads:
        load.start()
    wb[...] = jnp.zeros_like(wb)

    def near_dev(k):
        t = lax.rem(near + k, 8)
        return (chip * 2 + t // 4, lax.rem(t, 4)), t

    def far_dev(k):
        t = lax.rem(chip + k, 16)
        return (t * 2 + core, di), t

    barrier = pltpu.get_barrier_semaphore()
    greet = [far_dev(k)[0] for k in range(1, 16)]
    greet += [(a, b) for a in (up_s, dn_s) for b in (di, up_d, dn_d)]
    greet += [near_dev(k)[0] for k in range(1, 8)]
    for t in greet:
        pl.semaphore_signal(barrier, inc=1, device_id=t, device_id_type=MESH)

    for inside, planes, side in ((not_first_s, 0, 0), (not_last_s, S + 2, 1)):
        @pl.when(jnp.logical_not(inside))
        def _(planes=planes, side=side):
            for j in range(2):
                mb[planes + j] = jnp.zeros((D, N), f32)
                for c in range(C):
                    xb[c, planes + j] = jnp.zeros((D, N), f32)
                    for k in range(3):
                        ub[k, c, planes + j] = jnp.zeros((D, N), f32)
            for c in range(C):
                fb[c, (S + 1) * side] = jnp.zeros((D, N), f32)
            for j in range(6):
                coef[j, S + side] = jnp.zeros((D, N), f32)
            mc[side] = jnp.zeros((2, 8, N), f32)
            xc[side] = jnp.zeros((2, C, 8, N), f32)
            uc[side] = jnp.zeros((2, C, 8, N), f32)
    for inside, side in ((not_first_d, 0), (not_last_d, 1)):
        @pl.when(jnp.logical_not(inside))
        def _(side=side):
            for j in range(6):
                coef[j, S + 2 + side] = jnp.zeros((D, N), f32)
            mf[side] = jnp.zeros((2, S, N), f32)
            for c in range(C):
                xf[c, side] = jnp.zeros((2, S, N), f32)
                ff[c, side] = jnp.zeros((S, N), f32)
                for k in range(3):
                    uf[k, c, side] = jnp.zeros((2, S, N), f32)
            for a in range(2):
                mc[a, side] = jnp.zeros((8, N), f32)
                xc[a, side] = jnp.zeros((C, 8, N), f32)
                uc[a, side] = jnp.zeros((C, 8, N), f32)

    for load in loads[:3]:
        load.wait()
    owner = own[...]
    rows = owner.shape[1]
    same = (iota((128, rows), 0) == owner).astype(f32)
    before = (iota((rows, rows), 0) < iota((rows, rows), 1)).astype(f32).astype(bf16)
    count = jnp.dot(same.astype(bf16), before, preferred_element_type=f32)
    rank = jnp.sum(same * count, axis=0, keepdims=True)
    place = owner * CAP + rank.astype(i32)
    values = jnp.concatenate([mis[...], cel[...].astype(f32), jnp.zeros((4, rows), f32)], axis=0)
    parts = jnp.concatenate([p.astype(f32) for p in thirds(values)], axis=0).astype(bf16)

    def fill(q, _):
        hot = (iota((128, rows), 0) + (q * 64 - 32) == place).astype(f32)
        out = lax.dot_general(parts, hot.astype(bf16), (((1,), (1,)), ((), ())), preferred_element_type=f32)
        msg1[q] = (out[0:8] + out[8:16] + out[16:24])[0:4]
        return 0

    lax.fori_loop(0, 16, fill, 0, unroll=4)

    def stage(read, to, layers):
        for s in range(S):
            v = read(s)
            for layer in range(layers):
                to[0, layer, s:s + 1] = v[layer:layer + 1]
                to[1, layer, s:s + 1] = v[D - 1 - layer:D - layer]

    loads[3].wait()
    stage(lambda s: mb[s + 2], ms, 2)
    col = iota((D, 128), 1)
    for s in range(S):
        tile = mb[s + 2, :, 0:128]
        at = 4 * s + 16
        mask = (col >= at) & (col < at + 4)
        wb[1, 0, 8:24] += jnp.where(mask, pltpu.roll(tile, at, 1), 0.0)
        wb[1, 1, 8:24] += jnp.where(mask, pltpu.roll(tile, at - 1, 1), 0.0)
    loads[4].wait()
    for c in range(C):
        stage(lambda s, c=c: xb[c, s + 2], xs.at[c], 2)
    loads[5].wait()
    for c in range(C):
        for s in range(S):
            fs[c, 0, s:s + 1] = fb[c, s + 1, 0:1]
            fs[c, 1, s:s + 1] = fb[c, s + 1, D - 1:D]

    def remote(src, dst, send_sem, recv_sem, t):
        return pltpu.make_async_remote_copy(src_ref=src, dst_ref=dst, send_sem=send_sem, recv_sem=recv_sem,
                                            device_id=t, device_id_type=MESH)

    def edges(number, buf, face, edge):
        def sems(way):
            return ssem.at[number, way], rsem.at[number, way]
        return [
            (not_last_d, not_first_d, remote(edge.at[1], face.at[0], *sems(0), (si, up_d))),
            (not_first_d, not_last_d, remote(edge.at[0], face.at[1], *sems(1), (si, dn_d))),
            (not_last_s, not_first_s, remote(buf.at[pl.ds(S, 2)], buf.at[pl.ds(0, 2)], *sems(2), (up_s, di))),
            (not_first_s, not_last_s, remote(buf.at[pl.ds(2, 2)], buf.at[pl.ds(S + 2, 2)], *sems(3), (dn_s, di))),
        ]

    def forward_edges():
        def sems(way):
            return ssem.at[7, way], rsem.at[7, way]
        return [
            (not_last_d, not_first_d, remote(fs.at[:, 1], ff.at[:, 0], *sems(0), (si, up_d))),
            (not_first_d, not_last_d, remote(fs.at[:, 0], ff.at[:, 1], *sems(1), (si, dn_d))),
            (not_last_s, not_first_s, remote(fb.at[:, S], fb.at[:, 0], *sems(2), (up_s, di))),
            (not_first_s, not_last_s, remote(fb.at[:, 1], fb.at[:, S + 1], *sems(3), (dn_s, di))),
        ]

    ways = [(1, 1), (1, -1), (-1, 1), (-1, -1)]

    def reach(ps, pd):
        to_s, to_d = (not_last_s if ps > 0 else not_first_s), (not_last_d if pd > 0 else not_first_d)
        from_s, from_d = (not_first_s if ps > 0 else not_last_s), (not_first_d if pd > 0 else not_last_d)
        return to_s & to_d, from_s & from_d, (up_s if ps > 0 else dn_s, up_d if pd > 0 else dn_d)

    def corners(number, source, target):
        out = []
        for way, (ps, pd) in enumerate(ways):
            has, gets, t = reach(ps, pd)
            side, row = (1 if pd > 0 else 0), (S - 1 if ps > 0 else 0)
            a, b = (0 if ps > 0 else 1), (0 if pd > 0 else 1)
            out.append((has, gets, remote(source(side, row), target(a, b), cssem.at[number, way],
                                          crsem.at[number, way], t)))
        return out

    def patches():
        out = []
        for way, (ps, pd) in enumerate([(1, 0), (-1, 0), (0, 1), (0, -1)] + ways):
            if pd == 0:
                has, gets, t = (not_last_s, not_first_s, (up_s, di)) if ps > 0 else (not_first_s, not_last_s, (dn_s, di))
                src, dst = pl.ds(8, 16), pl.ds(8, 16)
            else:
                if ps == 0:
                    has, gets, t = (not_last_d, not_first_d, (si, up_d)) if pd > 0 else (not_first_d, not_last_d, (si, dn_d))
                else:
                    has, gets, t = reach(ps, pd)
                src, dst = (pl.ds(20, 4), pl.ds(4, 4)) if pd > 0 else (pl.ds(8, 4), pl.ds(24, 4))
            out.append((has, gets, remote(wb.at[1, :, src], wb.at[1 - ps, :, dst], wssem.at[way], wrsem.at[way], t)))
        return out

    def m_edges():
        return edges(0, mb, mf, ms) + corners(
            0, lambda side, row: ms.at[side, 0, pl.ds(row, 1)], lambda a, b: mc.at[a, b, pl.ds(0, 1)])

    def x_corners():
        return corners(1, lambda side, row: xs.at[:, side, 0, pl.ds(row, 1)], lambda a, b: xc.at[a, b, :, pl.ds(0, 1)])

    def x_edges(c):
        return edges(1 + c, xb.at[c], xf.at[c], xs.at[c])

    def u_edges(c):
        return edges(4 + c, ub.at[1, c], uf.at[1, c], us.at[c]) + corners(
            2 + c, lambda side, row: us.at[c, side, 0, pl.ds(row, 1)], lambda a, b: uc.at[a, b, c, pl.ds(0, 1)])

    def send(copies):
        for has, _, copy in copies:
            pl.when(has)(copy.start)

    def recv(copies):
        for _, gets, copy in copies:
            pl.when(gets)(copy.wait_recv)

    def sent(copies):
        for has, _, copy in copies:
            pl.when(has)(copy.wait_send)

    def row_copy(k):
        t, idx = far_dev(k)
        return remote(msg1.at[idx], got1.at[chip], s1.at[k], r1.at[k], t)

    def plane_copy(k):
        t, idx = near_dev(k)
        return remote(msg2.at[idx], got2.at[near], s2.at[k], r2.at[k], t)

    def sum_copy(k):
        t, _ = far_dev(k)
        return remote(red.at[0], got3.at[chip], s3.at[k], r3.at[k], t)

    def last_copy(k):
        t, _ = near_dev(k)
        return remote(red.at[1], got4.at[near], s4.at[k], r4.at[k], t)

    pl.semaphore_wait(barrier, len(greet))
    send(m_edges())
    send(x_corners())
    for c in range(C):
        send(x_edges(c))
        if c == 0:
            for k in range(1, 16):
                row_copy(k).start()
    send(patches())
    got1[chip] = msg1[chip]

    first, last = iota((D, N), 1) == 0, iota((D, N), 1) == N - 1

    def coefs(p, m, low, high, row_low, row_high):
        beside = [low, high, rows_low(m, row_low), rows_high(m, row_high),
                  jnp.where(first, 0.0, cols_low(m)), jnp.where(last, 0.0, cols_high(m))]
        face = [0.5 * (m + b) for b in beside]
        dd = jnp.where(first, PENALTY * m, 0.0)
        for a in face:
            dd = dd + a
        ii = 1.0 / dd
        for j in range(6):
            out = face[j] * ii
            if j == 4:
                out = jnp.where(first, 0.0, out)
            if j == 5:
                out = jnp.where(last, 0.0, out)
            coef[j, p] = out
        return dd

    recv(m_edges())

    def own_coefs(s, _):
        diag[s] = coefs(s, mb[s + 2], mb[s + 1], mb[s + 3], mf[0, 0, pl.ds(s, 1)], mf[1, 0, pl.ds(s, 1)])
        return 0

    lax.fori_loop(0, S, own_coefs, 0, unroll=2)
    outer = [not_first_s, not_last_s, not_first_d, not_last_d]

    def corner(cells, a, b):
        return cells(a, b)[0:1]

    def outer_planes(planes, faces, edge, cells):
        return [
            lambda: (planes(1), planes(0), planes(2), corner(cells, 0, 0), corner(cells, 0, 1)),
            lambda: (planes(S + 2), planes(S + 1), planes(S + 3), corner(cells, 1, 0), corner(cells, 1, 1)),
            lambda: (faces(0, 0), faces(0, 1), edge(0), corner(cells, 0, 0), corner(cells, 1, 0)),
            lambda: (faces(1, 0), edge(1), faces(1, 1), corner(cells, 0, 1), corner(cells, 1, 1)),
        ]

    for j, get in enumerate(outer_planes(lambda i: mb[i], lambda a, b: mf[a, b], lambda a: ms[a, 0],
                                         lambda a, b: mc[a, b])):
        @pl.when(outer[j])
        def _(j=j, get=get):
            coefs(S + j, *get())

    def sweep(p, v, low, high, row_low, row_high):
        out = coef[0, p] * low + coef[1, p] * high
        out = out + coef[2, p] * rows_low(v, row_low) + coef[3, p] * rows_high(v, row_high)
        return out + coef[4, p] * cols_low(v) + coef[5, p] * cols_high(v)

    def own_sweep(planes, faces, s):
        v = planes(s + 2)
        return v, sweep(s, v, planes(s + 1), planes(s + 3), faces(0, pl.ds(s, 1)), faces(1, pl.ds(s, 1)))

    def keep_outer(k, c, j, v):
        if j == 0:
            ub[k, c, 1] = v
        elif j == 1:
            ub[k, c, S + 2] = v
        else:
            uf[k, c, j - 2, 0] = v

    zero8 = jnp.zeros((8, 128), f32)
    sums0 = (zero8,) * 3
    sums1 = (zero8,) * 2
    sums2 = (zero8,)

    recv(x_corners())

    def first_half(c, sums):
        recv(x_edges(c))

        def start_field(s, _):
            v, w = own_sweep(lambda i: xb[c, i], lambda a, r: xf[c, a, 0, r], s)
            ub[0, c, s + 2] = w - v
            return 0

        lax.fori_loop(0, S, start_field, 0, unroll=UNROLL)
        for j, get in enumerate(outer_planes(lambda i: xb[c, i], lambda a, b: xf[c, a, b], lambda a: xs[c, a, 0],
                                             lambda a, b: xc[a, b, c])):
            got = get()
            keep_outer(0, c, j, sweep(S + j, *got) - got[0])

        def step(s, sums):
            v, w = own_sweep(lambda i: ub[0, c, i], lambda a, r: uf[0, c, a, 0, r], s)
            ub[1, c, s + 2] = w
            for layer in range(2):
                us[c, 0, layer, pl.ds(s, 1)] = w[layer:layer + 1]
                us[c, 1, layer, pl.ds(s, 1)] = w[D - 1 - layer:D - layer]
            dd = diag[s]
            de = dd * (v - w)
            return (sums[0] + fold(dd * v * v), sums[1] + fold(de * v), sums[2] + fold(de * w))

        sums = lax.fori_loop(0, S, step, sums, unroll=UNROLL)
        send(u_edges(c))
        return sums

    sums0 = first_half(0, sums0)

    for k in range(1, 16):
        row_copy(k).wait_recv()
    slot = iota((1, 128), 1)
    brick_s, brick_d = slot // 32 - 1, lax.rem(slot, 32) // CAP

    def plane_part(half, total):
        hot_d, right = [], [[], [], []]
        for j in range(4):
            row = got1[half * 4 + j]
            at = row[3:4].astype(i32)
            at_s, at_d = brick_s * S + at // D, brick_d * D + lax.rem(at, D) + 8
            hot_d.append((iota((80, 128), 0) == at_d).astype(f32))
            vals = [p.astype(f32) for p in thirds(row)]
            hits = [iota((32, 128), 0) == at_s + (4 - S * o) for o in range(2)]
            for part in range(3):
                lines = []
                for o in range(2):
                    for c in range(C):
                        lines.append(jnp.where(hits[o], vals[part][c:c + 1], 0.0))
                    lines.append(jnp.zeros((32, 128), f32))
                right[part].append(jnp.concatenate(lines, axis=0))
        left = jnp.concatenate(hot_d, axis=1).astype(bf16)
        for part in range(3):
            total = total + lax.dot_general(left, jnp.concatenate(right[part], axis=1).astype(bf16),
                                            (((1,), (1,)), ((), ())), preferred_element_type=f32)
        return total

    dense = jnp.zeros((80, 256), f32)
    for half in range(4):
        dense = plane_part(half, dense)
    for t in range(8):
        msg2[t] = dense[(t % 4) * D:(t % 4) * D + 32, (t // 4) * 128:(t // 4 + 1) * 128]
    for k in range(1, 8):
        plane_copy(k).start()
    got2[near] = msg2[near]

    for c in range(1, C):
        sums0 = first_half(c, sums0)
    send(forward_edges())

    recv(patches())
    lane = iota((32, 128), 1)

    def patch(a):
        low, mid, high = wb[0, a], wb[1, a], wb[2, a]
        return jnp.where(lane < 16, pltpu.roll(low, 64, 1), jnp.where(lane < 80, mid, jnp.where(
            lane < 96, pltpu.roll(high, 64, 1), 0.0)))

    m, above = patch(0), patch(1)
    layer = lax.rem(lane, 4)
    beside = [pltpu.roll(m, 4, 1), pltpu.roll(m, 124, 1), pltpu.roll(m, 1, 0), pltpu.roll(m, 31, 0),
              jnp.where(layer == 0, 0.0, pltpu.roll(m, 1, 1)), above]
    face = [0.5 * (m + b) for b in beside]
    total = jnp.where(layer == 0, PENALTY * m, 0.0)
    for a in face:
        total = total + a
    live = m > 0.0
    ii = jnp.where(live, 1.0 / jnp.where(live, total, 1.0), 0.0)
    face = [a * ii for a in face]
    face[4] = jnp.where(layer == 0, 0.0, face[4])
    face[5] = jnp.where(layer == 3, 0.0, face[5])

    def second_half(c, sums1, sums2):
        recv(u_edges(c))

        def step(s, sums):
            v, w = own_sweep(lambda i: ub[1, c, i], lambda a, r: uf[1, c, a, 0, r], s)
            ub[2, c, s + 2] = w
            de = diag[s] * (v - w)
            return (sums[0] + fold(de * v), sums[1] + fold(de * w))

        sums1 = lax.fori_loop(0, S, step, sums1, unroll=UNROLL)
        for j, get in enumerate(outer_planes(lambda i: ub[1, c, i], lambda a, b: uf[1, c, a, b],
                                             lambda a: us[c, a, 0], lambda a, b: uc[a, b, c])):
            keep_outer(2, c, j, sweep(S + j, *get()))

        def final(s, sums):
            v, w = own_sweep(lambda i: ub[2, c, i], lambda a, r: uf[2, c, a, 0, r], s)
            u3[c, s] = w[:, 0:128]
            return (sums[0] + fold(diag[s] * v * (v - w)),)

        sums2 = lax.fori_loop(0, S, final, sums2, unroll=UNROLL)
        return sums1, sums2

    for c in range(C):
        sums1, sums2 = second_half(c, sums1, sums2)

    for k in range(1, 8):
        plane_copy(k).wait_recv()
    plane = got2[0]
    for j in range(1, 8):
        plane = plane + got2[j]
    spread = ((iota((128, 384), 0) // 32 == iota((128, 384), 1) // 128)
              & (lax.rem(iota((128, 384), 0), 32) * 4 == lax.rem(iota((128, 384), 1), 128))).astype(f32).astype(bf16)
    left = jnp.concatenate([p.astype(f32) for p in thirds(plane)], axis=0).astype(bf16)
    out = jnp.dot(left, spread, preferred_element_type=f32)
    out = out[0:32] + out[32:64] + out[64:96]
    shares = [[out[:, 128 * c:128 * c + 128] * ii for c in range(C)]]
    for k in range(3):
        nxt = []
        for c in range(C):
            w = shares[k][c]
            nxt.append(face[0] * pltpu.roll(w, 4, 1) + face[1] * pltpu.roll(w, 124, 1)
                       + face[2] * pltpu.roll(w, 1, 0) + face[3] * pltpu.roll(w, 31, 0)
                       + face[4] * pltpu.roll(w, 1, 1) + face[5] * pltpu.roll(w, 127, 1))
        shares.append(nxt)

    few = col < 4

    def share(k, c, i):
        return jnp.where(few, pltpu.roll(shares[k][c][8:24], 128 - 4 * (i + 2), 1), 0.0)

    def fold_near(v):
        return v[0:8] + v[8:16]

    for c in range(C):
        sent(u_edges(c))
    sums0, sums1, sums2 = list(sums0), list(sums1), list(sums2)
    for s in range(S):
        dd = diag[s, :, 0:128]
        for c in range(C):
            v = []
            for k in range(3):
                v.append(ub[k, c, s + 2, :, 0:128] + share(k, c, s + 2))
                ub[k, c, s + 2, :, 0:128] = v[k]
            v.append(u3[c, s] + share(3, c, s + 2))
            de = [dd * (v[k] - v[k + 1]) for k in range(3)]
            sums0[0] = sums0[0] + fold_near(dd * v[0] * v[0])
            sums0[1] = sums0[1] + fold_near(de[0] * v[0])
            sums0[2] = sums0[2] + fold_near(de[0] * v[1])
            sums1[0] = sums1[0] + fold_near(de[1] * v[1])
            sums1[1] = sums1[1] + fold_near(de[1] * v[2])
            sums2[0] = sums2[0] + fold_near(de[2] * v[2])
    sums = sums0 + sums1 + sums2
    for j in range(6):
        red[0, j:j + 1] = jnp.sum(sums[j], axis=0, keepdims=True)
    red[0, 6:8] = jnp.zeros((2, 128), f32)

    for k in range(1, 16):
        sum_copy(k).start()
    got3[chip] = red[0]
    for k in range(3):
        for c in range(C):
            for i in (1, S + 2):
                ub[k, c, i, :, 0:128] += share(k, c, i)
            for side, r in ((0, 7), (1, 24)):
                row = jnp.broadcast_to(shares[k][c][r:r + 1], (S, 128))
                row = pltpu.roll(row, 128 - 16, 1)
                for bit in (1, 2, 4, 8):
                    row = jnp.where(iota((S, 128), 0) & bit > 0, pltpu.roll(row, 128 - 4 * bit, 1), row)
                uf[k, c, side, 0, :, 0:128] += jnp.where(few, row, 0.0)
    recv(forward_edges())

    start, end = iota((D, 128), 1) == 0, iota((D, 128), 1) == 127

    def cols_slope(v):
        tiles = [v[:, 128 * j:128 * j + 128] for j in range(4)]
        ups, downs = [pltpu.roll(t, 127, 1) for t in tiles], [pltpu.roll(t, 1, 1) for t in tiles]
        return jnp.concatenate([jnp.where(end, 0.0 if j == 3 else ups[min(j + 1, 3)], ups[j])
                                - jnp.where(start, 0.0 if j == 0 else downs[max(j - 1, 0)], downs[j])
                                for j in range(4)], 1)

    def slopes(p0, p1, p2, row_low, row_high):
        return p2 - p0, rows_high(p1, row_high) - rows_low(p1, row_low), cols_slope(p1)

    def gradients(s, _):
        total = [jnp.zeros((D, N), f32)] * 4
        for c in range(C):
            df = slopes(fb[c, s], fb[c, s + 1], fb[c, s + 2], ff[c, 0, pl.ds(s, 1)], ff[c, 1, pl.ds(s, 1)])
            for k in range(4):
                if k == 0:
                    buf, faces = xb.at[c], xf.at[c]
                else:
                    buf, faces = ub.at[k - 1, c], uf.at[k - 1, c]
                da = slopes(buf[s + 1], buf[s + 2], buf[s + 3], faces[0, 0, pl.ds(s, 1)], faces[1, 0, pl.ds(s, 1)])
                total[k] = total[k] + (df[0] * da[0] + df[1] * da[1] + df[2] * da[2])
        for k in range(4):
            gb[k, s] = -0.25 * total[k]
        return 0

    lax.fori_loop(0, S // 2, gradients, 0)
    for k in range(1, 16):
        sum_copy(k).wait_recv()
    part = got3[0]
    for j in range(1, 16):
        part = part + got3[j]
    red[1] = part
    for k in range(1, 8):
        last_copy(k).start()
    got4[near] = part
    lax.fori_loop(S // 2, S, gradients, 0)
    sent(m_edges())
    sent(x_corners())
    sent(patches())
    sent(forward_edges())
    for c in range(C):
        sent(x_edges(c))
    for k in range(1, 16):
        row_copy(k).wait_send()
        sum_copy(k).wait_send()
    for k in range(1, 8):
        plane_copy(k).wait_send()
    for k in range(1, 8):
        last_copy(k).wait_recv()
    part = got4[0]
    for j in range(1, 8):
        part = part + got4[j]
    tot = jnp.sum(part, axis=1, keepdims=True)

    b0, g0, g1, g2, g3, g4 = [tot[i:i + 1] for i in range(6)]
    b1 = b0 - g0
    b2 = b1 - g1
    l1, l2 = g1 / g0, g2 / g0
    s11, s12, s22 = g2 - l1 * g1, g3 - l1 * g2, g4 - l2 * g2
    y1, y2 = b1 - l1 * b0, b2 - l2 * b0
    l3 = s12 / s11
    c2 = (y2 - l3 * y1) / (s22 - l3 * s12)
    c1 = (y1 - s12 * c2) / s11
    c0 = (b0 - g1 * c1 - g2 * c2) / g0
    for j, v in enumerate((c0, c1, c2)):
        cv[j:j + 1] = jnp.broadcast_to(v, (1, 128))
    for k in range(1, 8):
        last_copy(k).wait_send()


CHUNK = 4


def finish(xb, ub, gb, cv, adj, grad, abuf, gout, sem):
    c = [cv[j:j + 1, 0:1] for j in range(3)]
    copies = []
    for part in range(S // CHUNK):
        for s in range(part * CHUNK, (part + 1) * CHUNK):
            for j in range(C):
                abuf[j, s] = xb[j, s + 2] + c[0] * ub[0, j, s + 2] + c[1] * ub[1, j, s + 2] + c[2] * ub[2, j, s + 2]
            gout[s] = gb[0, s] + c[0] * gb[1, s] + c[1] * gb[2, s] + c[2] * gb[3, s]
        at = pl.ds(part * CHUNK, CHUNK)
        copies.append(pltpu.make_async_copy(abuf.at[:, at], adj.at[:, at], sem.at[0, part]))
        copies.append(pltpu.make_async_copy(gout.at[at], grad.at[at], sem.at[1, part]))
        for copy in copies[-2:]:
            copy.start()
    for copy in copies:
        copy.wait()


def on_device(forward_field, adjoint_start, modulus, misfit, row_owner, row_cell):
    rows = row_cell.shape[0]
    vm, dma = pltpu.VMEM, pltpu.SemaphoreType.DMA
    hbm, inside = pl.BlockSpec(memory_space=pltpu.HBM), pl.BlockSpec(memory_space=pltpu.VMEM)
    shape = jax.ShapeDtypeStruct
    args = [pltpu.with_memory_space_constraint(a, pltpu.HBM) for a in (
        forward_field, adjoint_start, modulus, misfit, row_owner.reshape(1, rows), row_cell.reshape(1, rows))]
    kept = pl.pallas_call(
        window,
        out_shape=(vm((C, S + 4, D, N), f32), vm((3, C, S + 4, D, N), f32), vm((4, S, D, N), f32), vm((8, 128), f32)),
        in_specs=[hbm] * 6,
        out_specs=(inside,) * 4,
        scratch_shapes=[
            vm((S + 4, D, N), f32), vm((C, S + 2, D, N), f32),
            vm((2, 2, S, N), f32), vm((C, 2, 2, S, N), f32), vm((C, 2, S, N), f32), vm((3, C, 2, 2, S, N), f32),
            vm((2, 2, S, N), f32), vm((C, 2, 2, S, N), f32), vm((C, 2, S, N), f32), vm((C, 2, 2, S, N), f32),
            vm((2, 2, 8, N), f32), vm((2, 2, C, 8, N), f32), vm((2, 2, C, 8, N), f32),
            vm((6, S + 4, D, N), f32), vm((S, D, N), f32), vm((C, S, D, 128), f32), vm((3, 2, 32, 128), f32),
            vm((C, rows), f32), vm((1, rows), i32), vm((1, rows), i32),
            vm((16, 4, 128), f32), vm((16, 4, 128), f32), vm((8, 32, 128), f32), vm((8, 32, 128), f32),
            vm((2, 8, 128), f32), vm((16, 8, 128), f32), vm((8, 8, 128), f32),
            dma((6,)), dma((8, 4)), dma((8, 4)), dma((5, 4)), dma((5, 4)), dma((8,)), dma((8,)),
            dma((16,)), dma((16,)), dma((8,)), dma((8,)), dma((16,)), dma((16,)), dma((8,)), dma((8,)),
        ],
        compiler_params=pltpu.CompilerParams(collective_id=0, has_side_effects=True, vmem_limit_bytes=40 << 20),
        name="window",
    )(*args)
    return pl.pallas_call(
        finish,
        out_shape=(shape((C, S, D, N), f32), shape((S, D, N), f32)),
        in_specs=[inside] * 4,
        out_specs=(hbm, hbm),
        scratch_shapes=[vm((C, S, D, N), f32), vm((S, D, N), f32), dma((2, S // CHUNK))],
        compiler_params=pltpu.CompilerParams(vmem_limit_bytes=40 << 20),
        name="finish",
    )(*[pltpu.with_memory_space_constraint(a, pltpu.VMEM) for a in kept])


def solution(mesh):
    placed = (
        P(None, "strike", "depth", None),
        P(None, "strike", "depth", None),
        P("strike", "depth", None),
        P(None, ("strike", "depth")),
        P(("strike", "depth"), None),
        P(("strike", "depth")),
    )
    return jax.shard_map(
        on_device,
        mesh=mesh,
        in_specs=placed,
        out_specs=(P(None, "strike", "depth", None), P("strike", "depth", None)),
        check_vma=False,
    )
```

```python
import jax
import jax.numpy as jnp
from jax import lax
from jax.experimental import pallas as pl
from jax.experimental.pallas import tpu as pltpu
from jax.sharding import PartitionSpec as P

MESH = pl.DeviceIdType.MESH
C, S, D, N = 3, 16, 16, 512
NS_DEV, ND_DEV = 32, 4
CAP = 8
PENALTY = 4.0
f32, bf16, i32 = jnp.float32, jnp.bfloat16, jnp.int32
INNER, WHOLE = 14, 16


def iota(shape, dim):
    return lax.broadcasted_iota(i32, shape, dim)


def thirds(v):
    hi = v.astype(bf16)
    rest = v - hi.astype(f32)
    mid = rest.astype(bf16)
    return hi, mid, (rest - mid.astype(f32)).astype(bf16)


def cols_low(v):
    return pltpu.roll(v, 1, 1)


def cols_high(v):
    return pltpu.roll(v, N - 1, 1)


def rows_low(v, halo):
    row = iota((8, N), 0)
    top, low = pltpu.roll(v[0:8], 1, 0), pltpu.roll(v[8:16], 1, 0)
    return jnp.concatenate([jnp.where(row == 0, jnp.broadcast_to(halo, (8, N)), top), jnp.where(row == 0, top, low)], 0)


def rows_high(v, halo):
    row = iota((8, N), 0)
    top, low = pltpu.roll(v[0:8], 7, 0), pltpu.roll(v[8:16], 7, 0)
    return jnp.concatenate([jnp.where(row == 7, low, top), jnp.where(row == 7, jnp.broadcast_to(halo, (8, N)), low)], 0)


def fold(v):
    w = v[0:8] + v[8:16]
    return (w[:, 0:128] + w[:, 128:256]) + (w[:, 256:384] + w[:, 384:512])


def window(f_hbm, x_hbm, m_hbm, mis_hbm, own_hbm, cell_hbm, xb, ub, gb, cv,
           mb, fb, mf, xf, ff, uf, ms, xs, fs, us, mc, xc, uc, coef, diag, inv, u3, wb, mis, own, cel,
           msg1, got1, msg2, got2, red, got3, got4,
           load_sem, ssem, rsem, cssem, crsem, wssem, wrsem, s1, r1, s2, r2, s3, r3, s4, r4):
    si, di = lax.axis_index("strike"), lax.axis_index("depth")
    core, chip = lax.rem(si, 2), si // 2
    near = core * 4 + di
    up_s, dn_s = lax.rem(si + 1, NS_DEV), lax.rem(si + NS_DEV - 1, NS_DEV)
    up_d, dn_d = lax.rem(di + 1, ND_DEV), lax.rem(di + ND_DEV - 1, ND_DEV)
    not_first_s, not_last_s = si > 0, si < NS_DEV - 1
    not_first_d, not_last_d = di > 0, di < ND_DEV - 1

    loads = [pltpu.make_async_copy(src, dst, load_sem.at[j]) for j, (src, dst) in enumerate((
        (mis_hbm, mis), (own_hbm, own), (cell_hbm, cel), (m_hbm, mb.at[pl.ds(2, S)]), (x_hbm.at[0], xb.at[0, pl.ds(2, S)]), (x_hbm.at[1], xb.at[1, pl.ds(2, S)]),
        (x_hbm.at[2], xb.at[2, pl.ds(2, S)]), (f_hbm, fb.at[:, pl.ds(1, S)])))]
    for load in loads:
        load.start()
    wb[...] = jnp.zeros_like(wb)

    def near_dev(k):
        t = lax.rem(near + k, 8)
        return (chip * 2 + t // 4, lax.rem(t, 4)), t

    def far_dev(k):
        t = lax.rem(chip + k, 16)
        return (t * 2 + core, di), t

    barrier = pltpu.get_barrier_semaphore()
    greet = [far_dev(k)[0] for k in range(1, 16)]
    greet += [(a, b) for a in (up_s, dn_s) for b in (di, up_d, dn_d)]
    greet += [near_dev(k)[0] for k in range(1, 8)]
    for t in greet:
        pl.semaphore_signal(barrier, inc=1, device_id=t, device_id_type=MESH)

    def stage(read, to, layers):
        for g in range(0, S, 4):
            got = [read(s) for s in range(g, g + 4)]
            for j, v in enumerate(got):
                for layer in range(layers):
                    to[0, layer, g + j:g + j + 1] = v[layer:layer + 1]
                    to[1, layer, g + j:g + j + 1] = v[D - 1 - layer:D - layer]

    def remote(src, dst, send_sem, recv_sem, t):
        return pltpu.make_async_remote_copy(src_ref=src, dst_ref=dst, send_sem=send_sem, recv_sem=recv_sem,
                                            device_id=t, device_id_type=MESH)

    def edges(number, buf, face, edge):
        def sems(way):
            return ssem.at[number, way], rsem.at[number, way]
        return [
            (not_last_d, not_first_d, remote(edge.at[1], face.at[0], *sems(0), (si, up_d))),
            (not_first_d, not_last_d, remote(edge.at[0], face.at[1], *sems(1), (si, dn_d))),
            (not_last_s, not_first_s, remote(buf.at[pl.ds(S, 2)], buf.at[pl.ds(0, 2)], *sems(2), (up_s, di))),
            (not_first_s, not_last_s, remote(buf.at[pl.ds(2, 2)], buf.at[pl.ds(S + 2, 2)], *sems(3), (dn_s, di))),
        ]

    def forward_edges():
        def sems(way):
            return ssem.at[7, way], rsem.at[7, way]
        return [
            (not_last_d, not_first_d, remote(fs.at[:, 1], ff.at[:, 0], *sems(0), (si, up_d))),
            (not_first_d, not_last_d, remote(fs.at[:, 0], ff.at[:, 1], *sems(1), (si, dn_d))),
            (not_last_s, not_first_s, remote(fb.at[:, S], fb.at[:, 0], *sems(2), (up_s, di))),
            (not_first_s, not_last_s, remote(fb.at[:, 1], fb.at[:, S + 1], *sems(3), (dn_s, di))),
        ]

    ways = [(1, 1), (1, -1), (-1, 1), (-1, -1)]

    def reach(ps, pd):
        to_s, to_d = (not_last_s if ps > 0 else not_first_s), (not_last_d if pd > 0 else not_first_d)
        from_s, from_d = (not_first_s if ps > 0 else not_last_s), (not_first_d if pd > 0 else not_last_d)
        return to_s & to_d, from_s & from_d, (up_s if ps > 0 else dn_s, up_d if pd > 0 else dn_d)

    def corners(number, source, target):
        out = []
        for way, (ps, pd) in enumerate(ways):
            has, gets, t = reach(ps, pd)
            side, row = (1 if pd > 0 else 0), (S - 1 if ps > 0 else 0)
            a, b = (0 if ps > 0 else 1), (0 if pd > 0 else 1)
            out.append((has, gets, remote(source(side, row), target(a, b), cssem.at[number, way],
                                          crsem.at[number, way], t)))
        return out

    def patches():
        out = []
        for way, (ps, pd) in enumerate([(1, 0), (-1, 0), (0, 1), (0, -1)] + ways):
            if pd == 0:
                has, gets, t = (not_last_s, not_first_s, (up_s, di)) if ps > 0 else (not_first_s, not_last_s, (dn_s, di))
                src, dst = pl.ds(8, 16), pl.ds(8, 16)
            else:
                if ps == 0:
                    has, gets, t = (not_last_d, not_first_d, (si, up_d)) if pd > 0 else (not_first_d, not_last_d, (si, dn_d))
                else:
                    has, gets, t = reach(ps, pd)
                src, dst = (pl.ds(20, 4), pl.ds(4, 4)) if pd > 0 else (pl.ds(8, 4), pl.ds(24, 4))
            out.append((has, gets, remote(wb.at[1, :, src], wb.at[1 - ps, :, dst], wssem.at[way], wrsem.at[way], t)))
        return out

    def m_edges():
        return edges(0, mb, mf, ms) + corners(
            0, lambda side, row: ms.at[side, 0, pl.ds(row, 1)], lambda a, b: mc.at[a, b, pl.ds(0, 1)])

    def x_edges(c):
        return edges(1 + c, xb.at[c], xf.at[c], xs.at[c]) + corners(
            1 + c, lambda side, row: xs.at[c, side, 0, pl.ds(row, 1)], lambda a, b: xc.at[a, b, c, pl.ds(0, 1)])

    def u_edges(c):
        return edges(4 + c, ub.at[1, c], uf.at[1, c], us.at[c]) + corners(
            4 + c, lambda side, row: us.at[c, side, 0, pl.ds(row, 1)], lambda a, b: uc.at[a, b, c, pl.ds(0, 1)])

    def send(copies):
        for has, _, copy in copies:
            pl.when(has)(copy.start)

    def recv(copies):
        for _, gets, copy in copies:
            pl.when(gets)(copy.wait_recv)

    def sent(copies):
        for has, _, copy in copies:
            pl.when(has)(copy.wait_send)

    def row_copy(k):
        t, idx = far_dev(k)
        return remote(msg1.at[idx], got1.at[chip], s1.at[k], r1.at[k], t)

    def plane_copy(k):
        t, idx = near_dev(k)
        return remote(msg2.at[lax.rem(idx, 4)], got2.at[near], s2.at[k], r2.at[k], t)

    def sum_copy(k):
        t, _ = far_dev(k)
        return remote(red.at[0], got3.at[chip], s3.at[k], r3.at[k], t)

    def last_copy(k):
        t, _ = near_dev(k)
        return remote(red.at[1], got4.at[near], s4.at[k], r4.at[k], t)

    for load in loads[:3]:
        load.wait()
    owner = own[...]
    rows = owner.shape[1]
    same = (iota((128, rows), 0) == owner).astype(f32)
    before = (iota((rows, rows), 0) < iota((rows, rows), 1)).astype(f32).astype(bf16)
    count = jnp.dot(same.astype(bf16), before, preferred_element_type=f32)
    rank = jnp.sum(same * count, axis=0, keepdims=True)
    place = owner * CAP + rank.astype(i32)
    values = jnp.concatenate([mis[...], cel[...].astype(f32), jnp.zeros((4, rows), f32)], axis=0)
    parts = jnp.concatenate([p.astype(f32) for p in thirds(values)], axis=0).astype(bf16)

    def fill(q, _):
        hot = (iota((128, rows), 0) + (q * 64 - 32) == place).astype(f32)
        out = lax.dot_general(parts, hot.astype(bf16), (((1,), (1,)), ((), ())), preferred_element_type=f32)
        msg1[q] = (out[0:8] + out[8:16] + out[16:24])[0:4]
        return 0

    lax.fori_loop(0, 16, fill, 0, unroll=4)

    loads[3].wait()
    stage(lambda s: mb[s + 2], ms, 2)
    pl.semaphore_wait(barrier, len(greet))
    send(m_edges())
    for c in range(C):
        loads[4 + c].wait()
        stage(lambda s, c=c: xb[c, s + 2], xs.at[c], 2)
        send(x_edges(c))

    for k in range(1, 16):
        row_copy(k).start()
    got1[chip] = msg1[chip]
    col = iota((D, 128), 1)
    for s in range(S):
        tile = mb[s + 2, :, 0:128]
        at = 4 * s + 16
        mask = (col >= at) & (col < at + 4)
        wb[1, 0, 8:24] += jnp.where(mask, pltpu.roll(tile, at, 1), 0.0)
        wb[1, 1, 8:24] += jnp.where(mask, pltpu.roll(tile, at - 1, 1), 0.0)
    send(patches())

    for inside, planes, side in ((not_first_s, 0, 0), (not_last_s, S + 2, 1)):
        @pl.when(jnp.logical_not(inside))
        def _(planes=planes, side=side):
            for j in range(2):
                mb[planes + j] = jnp.zeros((D, N), f32)
                for c in range(C):
                    xb[c, planes + j] = jnp.zeros((D, N), f32)
                    for k in range(3):
                        ub[k, c, planes + j] = jnp.zeros((D, N), f32)
            for c in range(C):
                fb[c, (S + 1) * side] = jnp.zeros((D, N), f32)
            for j in range(6):
                coef[j, S + side] = jnp.zeros((D, N), f32)
            inv[S + side] = jnp.zeros((D, N), f32)
            mc[side] = jnp.zeros((2, 8, N), f32)
            xc[side] = jnp.zeros((2, C, 8, N), f32)
            uc[side] = jnp.zeros((2, C, 8, N), f32)
    for inside, side in ((not_first_d, 0), (not_last_d, 1)):
        @pl.when(jnp.logical_not(inside))
        def _(side=side):
            for j in range(6):
                coef[j, S + 2 + side] = jnp.zeros((D, N), f32)
            inv[S + 2 + side] = jnp.zeros((D, N), f32)
            mf[side] = jnp.zeros((2, S, N), f32)
            for c in range(C):
                xf[c, side] = jnp.zeros((2, S, N), f32)
                ff[c, side] = jnp.zeros((S, N), f32)
                for k in range(3):
                    uf[k, c, side] = jnp.zeros((2, S, N), f32)
            for a in range(2):
                mc[a, side] = jnp.zeros((8, N), f32)
                xc[a, side] = jnp.zeros((C, 8, N), f32)
                uc[a, side] = jnp.zeros((C, 8, N), f32)

    first, last = iota((D, N), 1) == 0, iota((D, N), 1) == N - 1
    none = jnp.zeros((D, N), f32)
    no_row = jnp.zeros((1, N), f32)

    def coefs(p, m, low, high, row_low, row_high):
        beside = [low, high, rows_low(m, row_low), rows_high(m, row_high), cols_low(m), cols_high(m)]
        face = [0.5 * (m + b) for b in beside]
        dd = jnp.where(first, PENALTY * m + 0.5 * m, face[4]) + jnp.where(last, 0.5 * m, face[5])
        for a in face[:4]:
            dd = dd + a
        for j in range(4):
            coef[j, p] = face[j]
        coef[4, p] = jnp.where(first, 0.0, face[4])
        coef[5, p] = jnp.where(last, 0.0, face[5])
        return dd

    def put_diag(s, dd):
        diag[s] = dd

    def part_coefs(s, low, high):
        return coefs(s, mb[s + 2], low, high, no_row, no_row)

    def inner(work, put):
        def step(g, _):
            at = [1 + g * INNER + j for j in range(INNER)]
            got = [work(s) for s in at]
            for s, v in zip(at, got):
                put(s, v)
            return 0
        lax.fori_loop(0, (S - 2) // INNER, step, 0)

    def summed(first_plane, planes, work, put, sums):
        group = WHOLE if planes == S else INNER

        def step(g, sums):
            at = [first_plane + g * group + j for j in range(group)]
            got = [work(s) for s in at]
            for s, (v, _) in zip(at, got):
                put(s, v)
            for _, terms in got:
                sums = tuple(a + fold(t) for a, t in zip(sums, terms))
            return sums
        return lax.fori_loop(0, planes // group, step, sums)

    put_diag(0, part_coefs(0, none, mb[3]))
    put_diag(S - 1, part_coefs(S - 1, mb[S], none))
    inner(lambda s: part_coefs(s, mb[s + 1], mb[s + 3]), put_diag)

    def sweep(p, v, low, high, row_low, row_high):
        out = coef[4, p] * cols_low(v) + coef[5, p] * cols_high(v)
        out = out + coef[2, p] * rows_low(v, row_low) + coef[3, p] * rows_high(v, row_high)
        if low is not None:
            out = out + coef[0, p] * low
        if high is not None:
            out = out + coef[1, p] * high
        return out

    def part_field(planes, put):
        put(0, sweep(0, planes(2), None, planes(3), no_row, no_row))
        put(S - 1, sweep(S - 1, planes(S + 1), planes(S), None, no_row, no_row))
        inner(lambda s: sweep(s, planes(s + 2), planes(s + 1), planes(s + 3), no_row, no_row), put)

    top, bottom = iota((8, N), 0) == 0, iota((8, N), 0) == 7

    def rest_of(s, w, faces, low, high):
        up = w[0:8] + jnp.where(top, coef[2, s, 0:8] * faces(0, pl.ds(s, 1)), 0.0)
        dn = w[8:16] + jnp.where(bottom, coef[3, s, 8:16] * faces(1, pl.ds(s, 1)), 0.0)
        w = jnp.concatenate([up, dn], 0)
        if low is not None:
            w = w + coef[0, s] * low
        if high is not None:
            w = w + coef[1, s] * high
        return w

    def put_part(k, c):
        def put(s, w):
            ub[k, c, s + 2] = w
        return put

    for c in range(C):
        part_field(lambda i, c=c: xb[c, i], put_part(0, c))

    recv(m_edges())

    def rest_coefs(s, low, high):
        up, dn = 0.5 * mf[0, 0, pl.ds(s, 1)], 0.5 * mf[1, 0, pl.ds(s, 1)]
        up, dn = jnp.where(top, up, 0.0), jnp.where(bottom, dn, 0.0)
        coef[2, s, 0:8] += up
        coef[3, s, 8:16] += dn
        dd = diag[s] + jnp.concatenate([up, dn], 0)
        for j, halo in ((0, low), (1, high)):
            if halo is not None:
                coef[j, s] += 0.5 * halo
                dd = dd + 0.5 * halo
        diag[s] = dd
        inv[s] = 1.0 / dd

    rest_coefs(0, mb[1], None)
    rest_coefs(S - 1, None, mb[S + 2])
    inner(lambda s: rest_coefs(s, None, None), lambda s, v: None)
    outer = [not_first_s, not_last_s, not_first_d, not_last_d]

    def corner(cells, a, b):
        return cells(a, b)[0:1]

    def outer_planes(planes, faces, edge, cells):
        return [
            lambda: (planes(1), planes(0), planes(2), corner(cells, 0, 0), corner(cells, 0, 1)),
            lambda: (planes(S + 2), planes(S + 1), planes(S + 3), corner(cells, 1, 0), corner(cells, 1, 1)),
            lambda: (faces(0, 0), faces(0, 1), edge(0), corner(cells, 0, 0), corner(cells, 1, 0)),
            lambda: (faces(1, 0), edge(1), faces(1, 1), corner(cells, 0, 1), corner(cells, 1, 1)),
        ]

    for j, get in enumerate(outer_planes(lambda i: mb[i], lambda a, b: mf[a, b], lambda a: ms[a, 0],
                                         lambda a, b: mc[a, b])):
        @pl.when(outer[j])
        def _(j=j, get=get):
            inv[S + j] = 1.0 / coefs(S + j, *get())

    def own_sweep(planes, faces, s):
        v = planes(s + 2)
        return v, inv[s] * sweep(s, v, planes(s + 1), planes(s + 3), faces(0, pl.ds(s, 1)), faces(1, pl.ds(s, 1)))

    def keep_outer(k, c, j, v):
        if j == 0:
            ub[k, c, 1] = v
        elif j == 1:
            ub[k, c, S + 2] = v
        else:
            uf[k, c, j - 2, 0] = v

    zero8 = jnp.zeros((8, 128), f32)
    sums0 = (zero8,) * 3
    sums1 = (zero8,) * 2
    sums2 = (zero8,)

    def first_half(c, sums):
        recv(x_edges(c))

        def start_field(s, low, high):
            w = rest_of(s, ub[0, c, s + 2], lambda a, r: xf[c, a, 0, r], low, high)
            return inv[s] * w - xb[c, s + 2]

        put = put_part(0, c)
        ends = start_field(0, xb[c, 1], None), start_field(S - 1, None, xb[c, S + 2])
        put(0, ends[0])
        put(S - 1, ends[1])
        inner(lambda s: start_field(s, None, None), put)
        made = []
        for j, get in enumerate(outer_planes(lambda i: xb[c, i], lambda a, b: xf[c, a, b], lambda a: xs[c, a, 0],
                                             lambda a, b: xc[a, b, c])):
            got = get()
            made.append(inv[S + j] * sweep(S + j, *got) - got[0])
        for j, v in enumerate(made):
            keep_outer(0, c, j, v)

        def step(s):
            v, w = own_sweep(lambda i: ub[0, c, i], lambda a, r: uf[0, c, a, 0, r], s)
            dd = diag[s]
            de = dd * (v - w)
            return w, (dd * v * v, de * v, de * w)

        def put_next(s, w):
            ub[1, c, s + 2] = w
            for layer in range(2):
                us[c, 0, layer, pl.ds(s, 1)] = w[layer:layer + 1]
                us[c, 1, layer, pl.ds(s, 1)] = w[D - 1 - layer:D - layer]

        sums = summed(0, S, step, put_next, sums)
        send(u_edges(c))
        return sums

    sums0 = first_half(0, sums0)

    for k in range(1, 16):
        row_copy(k).wait_recv()
    slot = iota((1, 128), 1)
    brick_s, brick_d = slot // 32 - 1, lax.rem(slot, 32) // CAP

    def plane_part(half, total):
        hot_d, right = [], [[], [], []]
        for j in range(4):
            row = got1[half * 4 + j]
            at = row[3:4].astype(i32)
            at_s, at_d = brick_s * S + at // D, brick_d * D + lax.rem(at, D) + 8
            hot_d.append((iota((80, 128), 0) == at_d).astype(f32))
            vals = [p.astype(f32) for p in thirds(row)]
            hit = iota((40, 128), 0) == at_s + 4
            for part in range(3):
                lines = [jnp.where(hit, vals[part][c:c + 1], 0.0) for c in range(C)] + [jnp.zeros((8, 128), f32)]
                right[part].append(jnp.concatenate(lines, axis=0))
        left = jnp.concatenate(hot_d, axis=1).astype(bf16)
        for part in range(3):
            total = total + lax.dot_general(left, jnp.concatenate(right[part], axis=1).astype(bf16),
                                            (((1,), (1,)), ((), ())), preferred_element_type=f32)
        return total

    dense = jnp.zeros((80, 128), f32)
    for half in range(4):
        dense = plane_part(half, dense)
    for t in range(4):
        msg2[t] = dense[t * D:t * D + 32]
    for k in range(1, 8):
        plane_copy(k).start()
    got2[near] = msg2[di]

    for c in range(1, C):
        sums0 = first_half(c, sums0)
    loads[7].wait()
    for c in range(C):
        for s in range(S):
            fs[c, 0, s:s + 1] = fb[c, s + 1, 0:1]
            fs[c, 1, s:s + 1] = fb[c, s + 1, D - 1:D]

    send(forward_edges())
    for c in range(C):
        part_field(lambda i, c=c: ub[1, c, i], put_part(2, c))

    recv(patches())
    lane = iota((32, 128), 1)

    def patch(a):
        low, mid, high = wb[0, a], wb[1, a], wb[2, a]
        return jnp.where(lane < 16, pltpu.roll(low, 64, 1), jnp.where(lane < 80, mid, jnp.where(
            lane < 96, pltpu.roll(high, 64, 1), 0.0)))

    m, above = patch(0), patch(1)
    layer = lax.rem(lane, 4)
    beside = [pltpu.roll(m, 4, 1), pltpu.roll(m, 124, 1), pltpu.roll(m, 1, 0), pltpu.roll(m, 31, 0),
              jnp.where(layer == 0, 0.0, pltpu.roll(m, 1, 1)), above]
    face = [0.5 * (m + b) for b in beside]
    total = jnp.where(layer == 0, PENALTY * m, 0.0)
    for a in face:
        total = total + a
    live = m > 0.0
    ii = jnp.where(live, 1.0 / jnp.where(live, total, 1.0), 0.0)
    face = [a * ii for a in face]
    face[4] = jnp.where(layer == 0, 0.0, face[4])
    face[5] = jnp.where(layer == 3, 0.0, face[5])

    def second_half(c, sums1, sums2):
        recv(u_edges(c))

        def step(s, low, high):
            v = ub[1, c, s + 2]
            w = inv[s] * rest_of(s, ub[2, c, s + 2], lambda a, r: uf[1, c, a, 0, r], low, high)
            de = diag[s] * (v - w)
            return w, (de * v, de * w)

        put = put_part(2, c)
        ends = step(0, ub[1, c, 1], None), step(S - 1, None, ub[1, c, S + 2])
        for s, (w, terms) in zip((0, S - 1), ends):
            put(s, w)
            sums1 = tuple(a + fold(t) for a, t in zip(sums1, terms))
        sums1 = summed(1, S - 2, lambda s: step(s, None, None), put, sums1)
        made = []
        for j, get in enumerate(outer_planes(lambda i: ub[1, c, i], lambda a, b: uf[1, c, a, b],
                                             lambda a: us[c, a, 0], lambda a, b: uc[a, b, c])):
            made.append(inv[S + j] * sweep(S + j, *get()))
        for j, v in enumerate(made):
            keep_outer(2, c, j, v)

        def final(s):
            v, w = own_sweep(lambda i: ub[2, c, i], lambda a, r: uf[2, c, a, 0, r], s)
            return w[:, 0:128], (diag[s] * v * (v - w),)

        def put_final(s, w):
            u3[c, s] = w

        sums2 = summed(0, S, final, put_final, sums2)
        return sums1, sums2

    for c in range(2):
        sums1, sums2 = second_half(c, sums1, sums2)

    for k in range(1, 8):
        plane_copy(k).wait_recv()
    plane = got2[0]
    for j in range(1, 8):
        plane = plane + got2[j]
    strike_at = lax.rem(iota((128, 128), 0), 40) - S * core
    spread = jnp.concatenate([
        ((iota((128, 128), 0) // 40 == c) & (strike_at < 24) & (strike_at * 4 == iota((128, 128), 1))).astype(f32)
        for c in range(C)], axis=1).astype(bf16)
    left = jnp.concatenate([p.astype(f32) for p in thirds(plane)], axis=0).astype(bf16)
    out = jnp.dot(left, spread, preferred_element_type=f32)
    out = out[0:32] + out[32:64] + out[64:96]
    shares = [[out[:, 128 * c:128 * c + 128] * ii for c in range(C)]]
    for k in range(3):
        nxt = []
        for c in range(C):
            w = shares[k][c]
            nxt.append(face[0] * pltpu.roll(w, 4, 1) + face[1] * pltpu.roll(w, 124, 1)
                       + face[2] * pltpu.roll(w, 1, 0) + face[3] * pltpu.roll(w, 31, 0)
                       + face[4] * pltpu.roll(w, 1, 1) + face[5] * pltpu.roll(w, 127, 1))
        shares.append(nxt)

    few = col < 4

    def share(k, c, i):
        return jnp.where(few, pltpu.roll(shares[k][c][8:24], 128 - 4 * (i + 2), 1), 0.0)

    def fold_near(v):
        return v[0:8] + v[8:16]

    weight = jnp.where((col >= 16) & (col < 80), total[8:24], 0.0)

    def gather(k, c):
        out = jnp.zeros((D, 128), f32)
        for s in range(S):
            tile = u3[c, s] if k == 3 else ub[k, c, s + 2, :, 0:128]
            out = jnp.where(col // 4 == s + 4, pltpu.roll(tile, 4 * s + 16, 1), out)
        return out

    def products(v):
        de = [weight * (v[k] - v[k + 1]) for k in range(3)]
        return [weight * v[0] * v[0], de[0] * v[0], de[0] * v[1], de[1] * v[1], de[1] * v[2], de[2] * v[2]]

    def change(c, sums):
        v = [gather(k, c) for k in range(4)]
        new = products([v[k] + shares[k][c][8:24] for k in range(4)])
        return [a + fold_near(p - q) for a, p, q in zip(sums, new, products(v))]

    sums = [zero8] * 6
    for c in range(2):
        sums = change(c, sums)
    sums1, sums2 = second_half(2, sums1, sums2)
    sums = change(2, sums)
    sums = [a + b for a, b in zip(sums, sums0 + sums1 + sums2)]
    for j in range(6):
        red[0, j:j + 1] = jnp.sum(sums[j], axis=0, keepdims=True)
    red[0, 6:8] = jnp.zeros((2, 128), f32)

    for k in range(1, 16):
        sum_copy(k).start()
    got3[chip] = red[0]
    for c in range(C):
        sent(u_edges(c))
    for k in range(3):
        for c in range(C):
            for g in range(1, S + 3, 18):
                new = [ub[k, c, i, :, 0:128] + share(k, c, i) for i in range(g, g + 18)]
                for j, v in enumerate(new):
                    ub[k, c, g + j, :, 0:128] = v

    @pl.when(si >= 0)
    def _():
        rows = []
        for k in range(3):
            for c in range(C):
                for side, r in ((0, 7), (1, 24)):
                    row = jnp.broadcast_to(shares[k][c][r:r + 1], (S, 128))
                    row = pltpu.roll(row, 128 - 16, 1)
                    for bit in (1, 2, 4, 8):
                        row = jnp.where(iota((S, 128), 0) & bit > 0, pltpu.roll(row, 128 - 4 * bit, 1), row)
                    rows.append(uf[k, c, side, 0, :, 0:128] + jnp.where(few, row, 0.0))
        for j, row in enumerate(rows):
            uf[j // (2 * C), (j // 2) % C, j % 2, 0, :, 0:128] = row

    recv(forward_edges())

    start, end = iota((D, 128), 1) == 0, iota((D, 128), 1) == 127

    def cols_slope(v):
        tiles = [v[:, 128 * j:128 * j + 128] for j in range(4)]
        ups, downs = [pltpu.roll(t, 127, 1) for t in tiles], [pltpu.roll(t, 1, 1) for t in tiles]
        return jnp.concatenate([jnp.where(end, 0.0 if j == 3 else ups[min(j + 1, 3)], ups[j])
                                - jnp.where(start, 0.0 if j == 0 else downs[max(j - 1, 0)], downs[j])
                                for j in range(4)], 1)

    def slopes(p0, p1, p2, row_low, row_high):
        return p2 - p0, rows_high(p1, row_high) - rows_low(p1, row_low), cols_slope(p1)

    def gradients(s, _):
        total = [jnp.zeros((D, N), f32)] * 4
        for c in range(C):
            df = slopes(fb[c, s], fb[c, s + 1], fb[c, s + 2], ff[c, 0, pl.ds(s, 1)], ff[c, 1, pl.ds(s, 1)])
            for k in range(4):
                if k == 0:
                    buf, faces = xb.at[c], xf.at[c]
                else:
                    buf, faces = ub.at[k - 1, c], uf.at[k - 1, c]
                da = slopes(buf[s + 1], buf[s + 2], buf[s + 3], faces[0, 0, pl.ds(s, 1)], faces[1, 0, pl.ds(s, 1)])
                total[k] = total[k] + (df[0] * da[0] + df[1] * da[1] + df[2] * da[2])
        for k in range(4):
            gb[k, s] = -0.25 * total[k]
        return 0

    lax.fori_loop(0, S // 2, gradients, 0, unroll=2)
    for k in range(1, 16):
        sum_copy(k).wait_recv()
    part = got3[0]
    for j in range(1, 16):
        part = part + got3[j]
    red[1] = part
    for k in range(1, 8):
        last_copy(k).start()
    got4[near] = part
    lax.fori_loop(S // 2, S, gradients, 0, unroll=2)
    sent(m_edges())
    sent(patches())
    sent(forward_edges())
    for c in range(C):
        sent(x_edges(c))
    for k in range(1, 16):
        row_copy(k).wait_send()
        sum_copy(k).wait_send()
    for k in range(1, 8):
        plane_copy(k).wait_send()
    for k in range(1, 8):
        last_copy(k).wait_recv()
    part = got4[0]
    for j in range(1, 8):
        part = part + got4[j]
    tot = jnp.sum(part, axis=1, keepdims=True)

    b0, g0, g1, g2, g3, g4 = [tot[i:i + 1] for i in range(6)]
    b1 = b0 - g0
    b2 = b1 - g1
    l1, l2 = g1 / g0, g2 / g0
    s11, s12, s22 = g2 - l1 * g1, g3 - l1 * g2, g4 - l2 * g2
    y1, y2 = b1 - l1 * b0, b2 - l2 * b0
    l3 = s12 / s11
    c2 = (y2 - l3 * y1) / (s22 - l3 * s12)
    c1 = (y1 - s12 * c2) / s11
    c0 = (b0 - g1 * c1 - g2 * c2) / g0
    for j, v in enumerate((c0, c1, c2)):
        cv[j:j + 1] = jnp.broadcast_to(v, (1, 128))
    for k in range(1, 8):
        last_copy(k).wait_send()


CHUNK = 4


def finish(xb, ub, gb, cv, adj, grad, abuf, gout, sem):
    c = [cv[j:j + 1, 0:1] for j in range(3)]
    copies = []
    for part in range(S // CHUNK):
        for s in range(part * CHUNK, (part + 1) * CHUNK):
            for j in range(C):
                abuf[j, s] = xb[j, s + 2] + c[0] * ub[0, j, s + 2] + c[1] * ub[1, j, s + 2] + c[2] * ub[2, j, s + 2]
            gout[s] = gb[0, s] + c[0] * gb[1, s] + c[1] * gb[2, s] + c[2] * gb[3, s]
        at = pl.ds(part * CHUNK, CHUNK)
        copies.append(pltpu.make_async_copy(abuf.at[:, at], adj.at[:, at], sem.at[0, part]))
        copies.append(pltpu.make_async_copy(gout.at[at], grad.at[at], sem.at[1, part]))
        for copy in copies[-2:]:
            copy.start()
    for copy in copies:
        copy.wait()


def on_device(forward_field, adjoint_start, modulus, misfit, row_owner, row_cell):
    rows = row_cell.shape[0]
    vm, dma = pltpu.VMEM, pltpu.SemaphoreType.DMA
    hbm, inside = pl.BlockSpec(memory_space=pltpu.HBM), pl.BlockSpec(memory_space=pltpu.VMEM)
    shape = jax.ShapeDtypeStruct
    args = [pltpu.with_memory_space_constraint(a, pltpu.HBM) for a in (
        forward_field, adjoint_start, modulus, misfit, row_owner.reshape(1, rows), row_cell.reshape(1, rows))]
    kept = pl.pallas_call(
        window,
        out_shape=(vm((C, S + 4, D, N), f32), vm((3, C, S + 4, D, N), f32), vm((4, S, D, N), f32), vm((8, 128), f32)),
        in_specs=[hbm] * 6,
        out_specs=(inside,) * 4,
        scratch_shapes=[
            vm((S + 4, D, N), f32), vm((C, S + 2, D, N), f32),
            vm((2, 2, S, N), f32), vm((C, 2, 2, S, N), f32), vm((C, 2, S, N), f32), vm((3, C, 2, 2, S, N), f32),
            vm((2, 2, S, N), f32), vm((C, 2, 2, S, N), f32), vm((C, 2, S, N), f32), vm((C, 2, 2, S, N), f32),
            vm((2, 2, 8, N), f32), vm((2, 2, C, 8, N), f32), vm((2, 2, C, 8, N), f32),
            vm((6, S + 4, D, N), f32), vm((S, D, N), f32), vm((S + 4, D, N), f32), vm((C, S, D, 128), f32), vm((3, 2, 32, 128), f32),
            vm((C, rows), f32), vm((1, rows), i32), vm((1, rows), i32),
            vm((16, 4, 128), f32), vm((16, 4, 128), f32), vm((4, 32, 128), f32), vm((8, 32, 128), f32),
            vm((2, 8, 128), f32), vm((16, 8, 128), f32), vm((8, 8, 128), f32),
            dma((8,)), dma((8, 4)), dma((8, 4)), dma((7, 4)), dma((7, 4)), dma((8,)), dma((8,)),
            dma((16,)), dma((16,)), dma((8,)), dma((8,)), dma((16,)), dma((16,)), dma((8,)), dma((8,)),
        ],
        compiler_params=pltpu.CompilerParams(collective_id=0, has_side_effects=True, vmem_limit_bytes=40 << 20),
        name="window",
    )(*args)
    return pl.pallas_call(
        finish,
        out_shape=(shape((C, S, D, N), f32), shape((S, D, N), f32)),
        in_specs=[inside] * 4,
        out_specs=(hbm, hbm),
        scratch_shapes=[vm((C, S, D, N), f32), vm((S, D, N), f32), dma((2, S // CHUNK))],
        compiler_params=pltpu.CompilerParams(vmem_limit_bytes=40 << 20),
        name="finish",
    )(*[pltpu.with_memory_space_constraint(a, pltpu.VMEM) for a in kept])


def solution(mesh):
    placed = (
        P(None, "strike", "depth", None),
        P(None, "strike", "depth", None),
        P("strike", "depth", None),
        P(None, ("strike", "depth")),
        P(("strike", "depth"), None),
        P(("strike", "depth")),
    )
    return jax.shard_map(
        on_device,
        mesh=mesh,
        in_specs=placed,
        out_specs=(P(None, "strike", "depth", None), P("strike", "depth", None)),
        check_vma=False,
    )
```

```python
import jax
import jax.numpy as jnp
from jax import lax
from jax.experimental import pallas as pl
from jax.experimental.pallas import tpu as pltpu
from jax.sharding import PartitionSpec as P

MESH = pl.DeviceIdType.MESH
C, S, D, N = 3, 16, 16, 512
NS_DEV, ND_DEV = 32, 4
CAP = 8
PENALTY = 4.0
f32, bf16, i32 = jnp.float32, jnp.bfloat16, jnp.int32
INNER, WHOLE = 14, 16


def iota(shape, dim):
    return lax.broadcasted_iota(i32, shape, dim)


def thirds(v):
    hi = v.astype(bf16)
    rest = v - hi.astype(f32)
    mid = rest.astype(bf16)
    return hi, mid, (rest - mid.astype(f32)).astype(bf16)


def cols_low(v):
    return pltpu.roll(v, 1, 1)


def cols_high(v):
    return pltpu.roll(v, N - 1, 1)


def rows_low(v, halo):
    row = iota((8, N), 0)
    top, low = pltpu.roll(v[0:8], 1, 0), pltpu.roll(v[8:16], 1, 0)
    return jnp.concatenate([jnp.where(row == 0, jnp.broadcast_to(halo, (8, N)), top), jnp.where(row == 0, top, low)], 0)


def rows_high(v, halo):
    row = iota((8, N), 0)
    top, low = pltpu.roll(v[0:8], 7, 0), pltpu.roll(v[8:16], 7, 0)
    return jnp.concatenate([jnp.where(row == 7, low, top), jnp.where(row == 7, jnp.broadcast_to(halo, (8, N)), low)], 0)


def fold(v):
    w = v[0:8] + v[8:16]
    return (w[:, 0:128] + w[:, 128:256]) + (w[:, 256:384] + w[:, 384:512])


def window(f_hbm, x_hbm, m_hbm, mis_hbm, own_hbm, cell_hbm, xb, ub, gb, cv,
           mb, fb, mf, xf, ff, uf, ms, xs, fs, us, mc, xc, uc, coef, diag, inv, u3, wb, mis, own, cel,
           msg1, got1, msg2, got2, red, got3, got4,
           load_sem, ssem, rsem, cssem, crsem, wssem, wrsem, s1, r1, s2, r2, s3, r3, s4, r4):
    si, di = lax.axis_index("strike"), lax.axis_index("depth")
    core, chip = lax.rem(si, 2), si // 2
    near = core * 4 + di
    up_s, dn_s = lax.rem(si + 1, NS_DEV), lax.rem(si + NS_DEV - 1, NS_DEV)
    up_d, dn_d = lax.rem(di + 1, ND_DEV), lax.rem(di + ND_DEV - 1, ND_DEV)
    not_first_s, not_last_s = si > 0, si < NS_DEV - 1
    not_first_d, not_last_d = di > 0, di < ND_DEV - 1

    loads = [pltpu.make_async_copy(src, dst, load_sem.at[j]) for j, (src, dst) in enumerate((
        (mis_hbm, mis), (own_hbm, own), (cell_hbm, cel), (m_hbm, mb.at[pl.ds(2, S)]), (x_hbm.at[0], xb.at[0, pl.ds(2, S)]), (x_hbm.at[1], xb.at[1, pl.ds(2, S)]),
        (x_hbm.at[2], xb.at[2, pl.ds(2, S)]), (f_hbm, fb.at[:, pl.ds(1, S)])))]
    for load in loads:
        load.start()
    wb[...] = jnp.zeros_like(wb)

    def near_dev(k):
        t = lax.rem(near + k, 8)
        return (chip * 2 + t // 4, lax.rem(t, 4)), t

    def far_dev(k):
        t = lax.rem(chip + k, 16)
        return (t * 2 + core, di), t

    barrier = pltpu.get_barrier_semaphore()
    greet = [far_dev(k)[0] for k in range(1, 16)]
    greet += [(a, b) for a in (up_s, dn_s) for b in (di, up_d, dn_d)]
    greet += [near_dev(k)[0] for k in range(1, 8)]
    for t in greet:
        pl.semaphore_signal(barrier, inc=1, device_id=t, device_id_type=MESH)

    def stage(read, to, layers):
        for g in range(0, S, 4):
            got = [read(s) for s in range(g, g + 4)]
            for j, v in enumerate(got):
                for layer in range(layers):
                    to[0, layer, g + j:g + j + 1] = v[layer:layer + 1]
                    to[1, layer, g + j:g + j + 1] = v[D - 1 - layer:D - layer]

    def remote(src, dst, send_sem, recv_sem, t):
        return pltpu.make_async_remote_copy(src_ref=src, dst_ref=dst, send_sem=send_sem, recv_sem=recv_sem,
                                            device_id=t, device_id_type=MESH)

    def edges(number, buf, face, edge):
        def sems(way):
            return ssem.at[number, way], rsem.at[number, way]
        return [
            (not_last_d, not_first_d, remote(edge.at[1], face.at[0], *sems(0), (si, up_d))),
            (not_first_d, not_last_d, remote(edge.at[0], face.at[1], *sems(1), (si, dn_d))),
            (not_last_s, not_first_s, remote(buf.at[pl.ds(S, 2)], buf.at[pl.ds(0, 2)], *sems(2), (up_s, di))),
            (not_first_s, not_last_s, remote(buf.at[pl.ds(2, 2)], buf.at[pl.ds(S + 2, 2)], *sems(3), (dn_s, di))),
        ]

    def forward_edges():
        def sems(way):
            return ssem.at[7, way], rsem.at[7, way]
        return [
            (not_last_d, not_first_d, remote(fs.at[:, 1], ff.at[:, 0], *sems(0), (si, up_d))),
            (not_first_d, not_last_d, remote(fs.at[:, 0], ff.at[:, 1], *sems(1), (si, dn_d))),
            (not_last_s, not_first_s, remote(fb.at[:, S], fb.at[:, 0], *sems(2), (up_s, di))),
            (not_first_s, not_last_s, remote(fb.at[:, 1], fb.at[:, S + 1], *sems(3), (dn_s, di))),
        ]

    ways = [(1, 1), (1, -1), (-1, 1), (-1, -1)]

    def reach(ps, pd):
        to_s, to_d = (not_last_s if ps > 0 else not_first_s), (not_last_d if pd > 0 else not_first_d)
        from_s, from_d = (not_first_s if ps > 0 else not_last_s), (not_first_d if pd > 0 else not_last_d)
        return to_s & to_d, from_s & from_d, (up_s if ps > 0 else dn_s, up_d if pd > 0 else dn_d)

    def corners(number, source, target):
        out = []
        for way, (ps, pd) in enumerate(ways):
            has, gets, t = reach(ps, pd)
            side, row = (1 if pd > 0 else 0), (S - 1 if ps > 0 else 0)
            a, b = (0 if ps > 0 else 1), (0 if pd > 0 else 1)
            out.append((has, gets, remote(source(side, row), target(a, b), cssem.at[number, way],
                                          crsem.at[number, way], t)))
        return out

    def patches():
        out = []
        for way, (ps, pd) in enumerate([(1, 0), (-1, 0), (0, 1), (0, -1)] + ways):
            if pd == 0:
                has, gets, t = (not_last_s, not_first_s, (up_s, di)) if ps > 0 else (not_first_s, not_last_s, (dn_s, di))
                src, dst = pl.ds(8, 16), pl.ds(8, 16)
            else:
                if ps == 0:
                    has, gets, t = (not_last_d, not_first_d, (si, up_d)) if pd > 0 else (not_first_d, not_last_d, (si, dn_d))
                else:
                    has, gets, t = reach(ps, pd)
                src, dst = (pl.ds(20, 4), pl.ds(4, 4)) if pd > 0 else (pl.ds(8, 4), pl.ds(24, 4))
            out.append((has, gets, remote(wb.at[1, :, src], wb.at[1 - ps, :, dst], wssem.at[way], wrsem.at[way], t)))
        return out

    def m_edges():
        return edges(0, mb, mf, ms) + corners(
            0, lambda side, row: ms.at[side, 0, pl.ds(row, 1)], lambda a, b: mc.at[a, b, pl.ds(0, 1)])

    def x_edges(c):
        return edges(1 + c, xb.at[c], xf.at[c], xs.at[c]) + corners(
            1 + c, lambda side, row: xs.at[c, side, 0, pl.ds(row, 1)], lambda a, b: xc.at[a, b, c, pl.ds(0, 1)])

    def u_edges(c):
        return edges(4 + c, ub.at[1, c], uf.at[1, c], us.at[c]) + corners(
            4 + c, lambda side, row: us.at[c, side, 0, pl.ds(row, 1)], lambda a, b: uc.at[a, b, c, pl.ds(0, 1)])

    def send(copies):
        for has, _, copy in copies:
            pl.when(has)(copy.start)

    def recv(copies):
        for _, gets, copy in copies:
            pl.when(gets)(copy.wait_recv)

    def sent(copies):
        for has, _, copy in copies:
            pl.when(has)(copy.wait_send)

    def row_copy(k):
        t, idx = far_dev(k)
        return remote(msg1.at[idx], got1.at[chip], s1.at[k], r1.at[k], t)

    def plane_copy(k):
        t, idx = near_dev(k)
        return remote(msg2.at[lax.rem(idx, 4)], got2.at[near], s2.at[k], r2.at[k], t)

    def sum_copy(k):
        t, _ = far_dev(k)
        return remote(red.at[0], got3.at[chip], s3.at[k], r3.at[k], t)

    def last_copy(k):
        t, _ = near_dev(k)
        return remote(red.at[1], got4.at[near], s4.at[k], r4.at[k], t)

    for load in loads[:3]:
        load.wait()
    owner = own[...]
    rows = owner.shape[1]
    same = (iota((128, rows), 0) == owner).astype(f32)
    before = (iota((rows, rows), 0) < iota((rows, rows), 1)).astype(f32).astype(bf16)
    count = jnp.dot(same.astype(bf16), before, preferred_element_type=f32)
    rank = jnp.sum(same * count, axis=0, keepdims=True)
    place = owner * CAP + rank.astype(i32)
    values = jnp.concatenate([mis[...], cel[...].astype(f32), jnp.zeros((4, rows), f32)], axis=0)
    parts = jnp.concatenate([p.astype(f32) for p in thirds(values)], axis=0).astype(bf16)

    def fill(q, _):
        hot = (iota((128, rows), 0) + (q * 64 - 32) == place).astype(f32)
        out = lax.dot_general(parts, hot.astype(bf16), (((1,), (1,)), ((), ())), preferred_element_type=f32)
        msg1[q] = (out[0:8] + out[8:16] + out[16:24])[0:4]
        return 0

    lax.fori_loop(0, 16, fill, 0, unroll=4)

    loads[3].wait()
    stage(lambda s: mb[s + 2], ms, 2)
    pl.semaphore_wait(barrier, len(greet))
    send(m_edges())
    for k in range(1, 16):
        row_copy(k).start()
    for c in range(C):
        loads[4 + c].wait()
        stage(lambda s, c=c: xb[c, s + 2], xs.at[c], 2)
        send(x_edges(c))

    got1[chip] = msg1[chip]
    col = iota((D, 128), 1)
    for s in range(S):
        tile = mb[s + 2, :, 0:128]
        at = 4 * s + 16
        mask = (col >= at) & (col < at + 4)
        wb[1, 0, 8:24] += jnp.where(mask, pltpu.roll(tile, at, 1), 0.0)
        wb[1, 1, 8:24] += jnp.where(mask, pltpu.roll(tile, at - 1, 1), 0.0)
    send(patches())

    for inside, planes, side in ((not_first_s, 0, 0), (not_last_s, S + 2, 1)):
        @pl.when(jnp.logical_not(inside))
        def _(planes=planes, side=side):
            for j in range(2):
                mb[planes + j] = jnp.zeros((D, N), f32)
                for c in range(C):
                    xb[c, planes + j] = jnp.zeros((D, N), f32)
                    for k in range(3):
                        ub[k, c, planes + j] = jnp.zeros((D, N), f32)
            for c in range(C):
                fb[c, (S + 1) * side] = jnp.zeros((D, N), f32)
            for j in range(6):
                coef[j, S + side] = jnp.zeros((D, N), f32)
            inv[S + side] = jnp.zeros((D, N), f32)
            mc[side] = jnp.zeros((2, 8, N), f32)
            xc[side] = jnp.zeros((2, C, 8, N), f32)
            uc[side] = jnp.zeros((2, C, 8, N), f32)
    for inside, side in ((not_first_d, 0), (not_last_d, 1)):
        @pl.when(jnp.logical_not(inside))
        def _(side=side):
            for j in range(6):
                coef[j, S + 2 + side] = jnp.zeros((D, N), f32)
            inv[S + 2 + side] = jnp.zeros((D, N), f32)
            mf[side] = jnp.zeros((2, S, N), f32)
            for c in range(C):
                xf[c, side] = jnp.zeros((2, S, N), f32)
                ff[c, side] = jnp.zeros((S, N), f32)
                for k in range(3):
                    uf[k, c, side] = jnp.zeros((2, S, N), f32)
            for a in range(2):
                mc[a, side] = jnp.zeros((8, N), f32)
                xc[a, side] = jnp.zeros((C, 8, N), f32)
                uc[a, side] = jnp.zeros((C, 8, N), f32)

    first, last = iota((D, N), 1) == 0, iota((D, N), 1) == N - 1
    none = jnp.zeros((D, N), f32)
    no_row = jnp.zeros((1, N), f32)

    def coefs(p, m, low, high, row_low, row_high):
        beside = [low, high, rows_low(m, row_low), rows_high(m, row_high), cols_low(m), cols_high(m)]
        face = [0.5 * (m + b) for b in beside]
        dd = jnp.where(first, PENALTY * m + 0.5 * m, face[4]) + jnp.where(last, 0.5 * m, face[5])
        for a in face[:4]:
            dd = dd + a
        for j in range(4):
            coef[j, p] = face[j]
        coef[4, p] = jnp.where(first, 0.0, face[4])
        coef[5, p] = jnp.where(last, 0.0, face[5])
        return dd

    def put_diag(s, dd):
        diag[s] = dd

    def part_coefs(s, low, high):
        return coefs(s, mb[s + 2], low, high, no_row, no_row)

    def inner(work, put):
        def step(g, _):
            at = [1 + g * INNER + j for j in range(INNER)]
            got = [work(s) for s in at]
            for s, v in zip(at, got):
                put(s, v)
            return 0
        lax.fori_loop(0, (S - 2) // INNER, step, 0)

    def summed(first_plane, planes, work, put, sums):
        group = WHOLE if planes == S else INNER

        def step(g, sums):
            at = [first_plane + g * group + j for j in range(group)]
            got = [work(s) for s in at]
            for s, (v, _) in zip(at, got):
                put(s, v)
            for _, terms in got:
                sums = tuple(a + fold(t) for a, t in zip(sums, terms))
            return sums
        return lax.fori_loop(0, planes // group, step, sums)

    put_diag(0, part_coefs(0, none, mb[3]))
    put_diag(S - 1, part_coefs(S - 1, mb[S], none))
    inner(lambda s: part_coefs(s, mb[s + 1], mb[s + 3]), put_diag)

    def sweep(p, v, low, high, row_low, row_high):
        out = coef[4, p] * cols_low(v) + coef[5, p] * cols_high(v)
        out = out + coef[2, p] * rows_low(v, row_low) + coef[3, p] * rows_high(v, row_high)
        if low is not None:
            out = out + coef[0, p] * low
        if high is not None:
            out = out + coef[1, p] * high
        return out

    def part_field(planes, put):
        put(0, sweep(0, planes(2), None, planes(3), no_row, no_row))
        put(S - 1, sweep(S - 1, planes(S + 1), planes(S), None, no_row, no_row))
        inner(lambda s: sweep(s, planes(s + 2), planes(s + 1), planes(s + 3), no_row, no_row), put)

    top, bottom = iota((8, N), 0) == 0, iota((8, N), 0) == 7

    def rest_of(s, w, faces, low, high):
        up = w[0:8] + jnp.where(top, coef[2, s, 0:8] * faces(0, pl.ds(s, 1)), 0.0)
        dn = w[8:16] + jnp.where(bottom, coef[3, s, 8:16] * faces(1, pl.ds(s, 1)), 0.0)
        w = jnp.concatenate([up, dn], 0)
        if low is not None:
            w = w + coef[0, s] * low
        if high is not None:
            w = w + coef[1, s] * high
        return w

    def put_part(k, c):
        def put(s, w):
            ub[k, c, s + 2] = w
        return put

    for c in range(C):
        part_field(lambda i, c=c: xb[c, i], put_part(0, c))

    recv(m_edges())

    def rest_coefs(s, low, high):
        up, dn = 0.5 * mf[0, 0, pl.ds(s, 1)], 0.5 * mf[1, 0, pl.ds(s, 1)]
        up, dn = jnp.where(top, up, 0.0), jnp.where(bottom, dn, 0.0)
        coef[2, s, 0:8] += up
        coef[3, s, 8:16] += dn
        dd = diag[s] + jnp.concatenate([up, dn], 0)
        for j, halo in ((0, low), (1, high)):
            if halo is not None:
                coef[j, s] += 0.5 * halo
                dd = dd + 0.5 * halo
        diag[s] = dd
        inv[s] = 1.0 / dd

    rest_coefs(0, mb[1], None)
    rest_coefs(S - 1, None, mb[S + 2])
    inner(lambda s: rest_coefs(s, None, None), lambda s, v: None)
    outer = [not_first_s, not_last_s, not_first_d, not_last_d]

    def corner(cells, a, b):
        return cells(a, b)[0:1]

    def outer_planes(planes, faces, edge, cells):
        return [
            lambda: (planes(1), planes(0), planes(2), corner(cells, 0, 0), corner(cells, 0, 1)),
            lambda: (planes(S + 2), planes(S + 1), planes(S + 3), corner(cells, 1, 0), corner(cells, 1, 1)),
            lambda: (faces(0, 0), faces(0, 1), edge(0), corner(cells, 0, 0), corner(cells, 1, 0)),
            lambda: (faces(1, 0), edge(1), faces(1, 1), corner(cells, 0, 1), corner(cells, 1, 1)),
        ]

    for j, get in enumerate(outer_planes(lambda i: mb[i], lambda a, b: mf[a, b], lambda a: ms[a, 0],
                                         lambda a, b: mc[a, b])):
        @pl.when(outer[j])
        def _(j=j, get=get):
            inv[S + j] = 1.0 / coefs(S + j, *get())

    def own_sweep(planes, faces, s):
        v = planes(s + 2)
        return v, inv[s] * sweep(s, v, planes(s + 1), planes(s + 3), faces(0, pl.ds(s, 1)), faces(1, pl.ds(s, 1)))

    def keep_outer(k, c, j, v):
        if j == 0:
            ub[k, c, 1] = v
        elif j == 1:
            ub[k, c, S + 2] = v
        else:
            uf[k, c, j - 2, 0] = v

    zero8 = jnp.zeros((8, 128), f32)
    sums0 = (zero8,) * 3
    sums1 = (zero8,) * 2
    sums2 = (zero8,)

    def first_half(c, sums):
        recv(x_edges(c))

        def start_field(s, low, high):
            w = rest_of(s, ub[0, c, s + 2], lambda a, r: xf[c, a, 0, r], low, high)
            return inv[s] * w - xb[c, s + 2]

        put = put_part(0, c)
        ends = start_field(0, xb[c, 1], None), start_field(S - 1, None, xb[c, S + 2])
        put(0, ends[0])
        put(S - 1, ends[1])
        inner(lambda s: start_field(s, None, None), put)
        made = []
        for j, get in enumerate(outer_planes(lambda i: xb[c, i], lambda a, b: xf[c, a, b], lambda a: xs[c, a, 0],
                                             lambda a, b: xc[a, b, c])):
            got = get()
            made.append(inv[S + j] * sweep(S + j, *got) - got[0])
        for j, v in enumerate(made):
            keep_outer(0, c, j, v)

        def step(s):
            v, w = own_sweep(lambda i: ub[0, c, i], lambda a, r: uf[0, c, a, 0, r], s)
            dd = diag[s]
            de = dd * (v - w)
            return w, (dd * v * v, de * v, de * w)

        def put_next(s, w):
            ub[1, c, s + 2] = w
            for layer in range(2):
                us[c, 0, layer, pl.ds(s, 1)] = w[layer:layer + 1]
                us[c, 1, layer, pl.ds(s, 1)] = w[D - 1 - layer:D - layer]

        sums = summed(0, S, step, put_next, sums)
        send(u_edges(c))
        return sums

    sums0 = first_half(0, sums0)

    for k in range(1, 16):
        row_copy(k).wait_recv()
    slot = iota((1, 128), 1)
    brick_s, brick_d = slot // 32 - 1, lax.rem(slot, 32) // CAP

    def plane_part(half, total):
        hot_d, right = [], [[], [], []]
        for j in range(4):
            row = got1[half * 4 + j]
            at = row[3:4].astype(i32)
            at_s, at_d = brick_s * S + at // D, brick_d * D + lax.rem(at, D) + 8
            hot_d.append((iota((80, 128), 0) == at_d).astype(f32))
            vals = [p.astype(f32) for p in thirds(row)]
            hit = iota((40, 128), 0) == at_s + 4
            for part in range(3):
                lines = [jnp.where(hit, vals[part][c:c + 1], 0.0) for c in range(C)] + [jnp.zeros((8, 128), f32)]
                right[part].append(jnp.concatenate(lines, axis=0))
        left = jnp.concatenate(hot_d, axis=1).astype(bf16)
        for part in range(3):
            total = total + lax.dot_general(left, jnp.concatenate(right[part], axis=1).astype(bf16),
                                            (((1,), (1,)), ((), ())), preferred_element_type=f32)
        return total

    dense = jnp.zeros((80, 128), f32)
    for half in range(4):
        dense = plane_part(half, dense)
    for t in range(4):
        msg2[t] = dense[t * D:t * D + 32]
    for k in range(1, 8):
        plane_copy(k).start()
    got2[near] = msg2[di]

    for c in range(1, C):
        sums0 = first_half(c, sums0)
    loads[7].wait()
    for c in range(C):
        for s in range(S):
            fs[c, 0, s:s + 1] = fb[c, s + 1, 0:1]
            fs[c, 1, s:s + 1] = fb[c, s + 1, D - 1:D]

    send(forward_edges())
    for c in range(C):
        part_field(lambda i, c=c: ub[1, c, i], put_part(2, c))

    recv(patches())
    lane = iota((32, 128), 1)

    def patch(a):
        low, mid, high = wb[0, a], wb[1, a], wb[2, a]
        return jnp.where(lane < 16, pltpu.roll(low, 64, 1), jnp.where(lane < 80, mid, jnp.where(
            lane < 96, pltpu.roll(high, 64, 1), 0.0)))

    m, above = patch(0), patch(1)
    layer = lax.rem(lane, 4)
    beside = [pltpu.roll(m, 4, 1), pltpu.roll(m, 124, 1), pltpu.roll(m, 1, 0), pltpu.roll(m, 31, 0),
              jnp.where(layer == 0, 0.0, pltpu.roll(m, 1, 1)), above]
    face = [0.5 * (m + b) for b in beside]
    total = jnp.where(layer == 0, PENALTY * m, 0.0)
    for a in face:
        total = total + a
    live = m > 0.0
    ii = jnp.where(live, 1.0 / jnp.where(live, total, 1.0), 0.0)
    face = [a * ii for a in face]
    face[4] = jnp.where(layer == 0, 0.0, face[4])
    face[5] = jnp.where(layer == 3, 0.0, face[5])

    def second_half(c, sums1, sums2):
        recv(u_edges(c))

        def step(s, low, high):
            v = ub[1, c, s + 2]
            w = inv[s] * rest_of(s, ub[2, c, s + 2], lambda a, r: uf[1, c, a, 0, r], low, high)
            de = diag[s] * (v - w)
            return w, (de * v, de * w)

        put = put_part(2, c)
        ends = step(0, ub[1, c, 1], None), step(S - 1, None, ub[1, c, S + 2])
        for s, (w, terms) in zip((0, S - 1), ends):
            put(s, w)
            sums1 = tuple(a + fold(t) for a, t in zip(sums1, terms))
        sums1 = summed(1, S - 2, lambda s: step(s, None, None), put, sums1)
        made = []
        for j, get in enumerate(outer_planes(lambda i: ub[1, c, i], lambda a, b: uf[1, c, a, b],
                                             lambda a: us[c, a, 0], lambda a, b: uc[a, b, c])):
            made.append(inv[S + j] * sweep(S + j, *get()))
        for j, v in enumerate(made):
            keep_outer(2, c, j, v)

        def final(s):
            v, w = own_sweep(lambda i: ub[2, c, i], lambda a, r: uf[2, c, a, 0, r], s)
            return w[:, 0:128], (diag[s] * v * (v - w),)

        def put_final(s, w):
            u3[c, s] = w

        sums2 = summed(0, S, final, put_final, sums2)
        return sums1, sums2

    for c in range(2):
        sums1, sums2 = second_half(c, sums1, sums2)

    for k in range(1, 8):
        plane_copy(k).wait_recv()
    plane = got2[0]
    for j in range(1, 8):
        plane = plane + got2[j]
    strike_at = lax.rem(iota((128, 128), 0), 40) - S * core
    spread = jnp.concatenate([
        ((iota((128, 128), 0) // 40 == c) & (strike_at < 24) & (strike_at * 4 == iota((128, 128), 1))).astype(f32)
        for c in range(C)], axis=1).astype(bf16)
    left = jnp.concatenate([p.astype(f32) for p in thirds(plane)], axis=0).astype(bf16)
    out = jnp.dot(left, spread, preferred_element_type=f32)
    out = out[0:32] + out[32:64] + out[64:96]
    shares = [[out[:, 128 * c:128 * c + 128] * ii for c in range(C)]]
    for k in range(3):
        nxt = []
        for c in range(C):
            w = shares[k][c]
            nxt.append(face[0] * pltpu.roll(w, 4, 1) + face[1] * pltpu.roll(w, 124, 1)
                       + face[2] * pltpu.roll(w, 1, 0) + face[3] * pltpu.roll(w, 31, 0)
                       + face[4] * pltpu.roll(w, 1, 1) + face[5] * pltpu.roll(w, 127, 1))
        shares.append(nxt)

    few = col < 4

    def share(k, c, i):
        return jnp.where(few, pltpu.roll(shares[k][c][8:24], 128 - 4 * (i + 2), 1), 0.0)

    def fold_near(v):
        return v[0:8] + v[8:16]

    weight = jnp.where((col >= 16) & (col < 80), total[8:24], 0.0)

    def gather(k, c):
        out = jnp.zeros((D, 128), f32)
        for s in range(S):
            tile = u3[c, s] if k == 3 else ub[k, c, s + 2, :, 0:128]
            out = jnp.where(col // 4 == s + 4, pltpu.roll(tile, 4 * s + 16, 1), out)
        return out

    def products(v):
        de = [weight * (v[k] - v[k + 1]) for k in range(3)]
        return [weight * v[0] * v[0], de[0] * v[0], de[0] * v[1], de[1] * v[1], de[1] * v[2], de[2] * v[2]]

    def change(c, sums):
        v = [gather(k, c) for k in range(4)]
        new = products([v[k] + shares[k][c][8:24] for k in range(4)])
        return [a + fold_near(p - q) for a, p, q in zip(sums, new, products(v))]

    sums = [zero8] * 6
    for c in range(2):
        sums = change(c, sums)
    sums1, sums2 = second_half(2, sums1, sums2)
    sums = change(2, sums)
    sums = [a + b for a, b in zip(sums, sums0 + sums1 + sums2)]
    for j in range(6):
        red[0, j:j + 1] = jnp.sum(sums[j], axis=0, keepdims=True)
    red[0, 6:8] = jnp.zeros((2, 128), f32)

    for k in range(1, 16):
        sum_copy(k).start()
    got3[chip] = red[0]
    for c in range(C):
        sent(u_edges(c))
    for k in range(3):
        for c in range(C):
            for g in range(1, S + 3, 18):
                new = [ub[k, c, i, :, 0:128] + share(k, c, i) for i in range(g, g + 18)]
                for j, v in enumerate(new):
                    ub[k, c, g + j, :, 0:128] = v

    @pl.when(si >= 0)
    def _():
        rows = []
        for k in range(3):
            for c in range(C):
                for side, r in ((0, 7), (1, 24)):
                    row = jnp.broadcast_to(shares[k][c][r:r + 1], (S, 128))
                    row = pltpu.roll(row, 128 - 16, 1)
                    for bit in (1, 2, 4, 8):
                        row = jnp.where(iota((S, 128), 0) & bit > 0, pltpu.roll(row, 128 - 4 * bit, 1), row)
                    rows.append(uf[k, c, side, 0, :, 0:128] + jnp.where(few, row, 0.0))
        for j, row in enumerate(rows):
            uf[j // (2 * C), (j // 2) % C, j % 2, 0, :, 0:128] = row

    recv(forward_edges())

    start, end = iota((D, 128), 1) == 0, iota((D, 128), 1) == 127

    def cols_slope(v):
        tiles = [v[:, 128 * j:128 * j + 128] for j in range(4)]
        ups, downs = [pltpu.roll(t, 127, 1) for t in tiles], [pltpu.roll(t, 1, 1) for t in tiles]
        return jnp.concatenate([jnp.where(end, 0.0 if j == 3 else ups[min(j + 1, 3)], ups[j])
                                - jnp.where(start, 0.0 if j == 0 else downs[max(j - 1, 0)], downs[j])
                                for j in range(4)], 1)

    def slopes(p0, p1, p2, row_low, row_high):
        return p2 - p0, rows_high(p1, row_high) - rows_low(p1, row_low), cols_slope(p1)

    def gradients(s, _):
        total = [jnp.zeros((D, N), f32)] * 4
        for c in range(C):
            df = slopes(fb[c, s], fb[c, s + 1], fb[c, s + 2], ff[c, 0, pl.ds(s, 1)], ff[c, 1, pl.ds(s, 1)])
            for k in range(4):
                if k == 0:
                    buf, faces = xb.at[c], xf.at[c]
                else:
                    buf, faces = ub.at[k - 1, c], uf.at[k - 1, c]
                da = slopes(buf[s + 1], buf[s + 2], buf[s + 3], faces[0, 0, pl.ds(s, 1)], faces[1, 0, pl.ds(s, 1)])
                total[k] = total[k] + (df[0] * da[0] + df[1] * da[1] + df[2] * da[2])
        for k in range(4):
            gb[k, s] = -0.25 * total[k]
        return 0

    lax.fori_loop(0, S // 2, gradients, 0, unroll=2)
    for k in range(1, 16):
        sum_copy(k).wait_recv()
    part = got3[0]
    for j in range(1, 16):
        part = part + got3[j]
    red[1] = part
    for k in range(1, 8):
        last_copy(k).start()
    got4[near] = part
    lax.fori_loop(S // 2, S, gradients, 0, unroll=2)
    sent(m_edges())
    sent(patches())
    sent(forward_edges())
    for c in range(C):
        sent(x_edges(c))
    for k in range(1, 16):
        row_copy(k).wait_send()
        sum_copy(k).wait_send()
    for k in range(1, 8):
        plane_copy(k).wait_send()
    for k in range(1, 8):
        last_copy(k).wait_recv()
    part = got4[0]
    for j in range(1, 8):
        part = part + got4[j]
    tot = jnp.sum(part, axis=1, keepdims=True)

    b0, g0, g1, g2, g3, g4 = [tot[i:i + 1] for i in range(6)]
    b1 = b0 - g0
    b2 = b1 - g1
    l1, l2 = g1 / g0, g2 / g0
    s11, s12, s22 = g2 - l1 * g1, g3 - l1 * g2, g4 - l2 * g2
    y1, y2 = b1 - l1 * b0, b2 - l2 * b0
    l3 = s12 / s11
    c2 = (y2 - l3 * y1) / (s22 - l3 * s12)
    c1 = (y1 - s12 * c2) / s11
    c0 = (b0 - g1 * c1 - g2 * c2) / g0
    for j, v in enumerate((c0, c1, c2)):
        cv[j:j + 1] = jnp.broadcast_to(v, (1, 128))
    for k in range(1, 8):
        last_copy(k).wait_send()


CHUNK = 4


def finish(xb, ub, gb, cv, adj, grad, abuf, gout, sem):
    c = [cv[j:j + 1, 0:1] for j in range(3)]
    copies = []
    for part in range(S // CHUNK):
        for s in range(part * CHUNK, (part + 1) * CHUNK):
            for j in range(C):
                abuf[j, s] = xb[j, s + 2] + c[0] * ub[0, j, s + 2] + c[1] * ub[1, j, s + 2] + c[2] * ub[2, j, s + 2]
            gout[s] = gb[0, s] + c[0] * gb[1, s] + c[1] * gb[2, s] + c[2] * gb[3, s]
        at = pl.ds(part * CHUNK, CHUNK)
        copies.append(pltpu.make_async_copy(abuf.at[:, at], adj.at[:, at], sem.at[0, part]))
        copies.append(pltpu.make_async_copy(gout.at[at], grad.at[at], sem.at[1, part]))
        for copy in copies[-2:]:
            copy.start()
    for copy in copies:
        copy.wait()


def on_device(forward_field, adjoint_start, modulus, misfit, row_owner, row_cell):
    rows = row_cell.shape[0]
    vm, dma = pltpu.VMEM, pltpu.SemaphoreType.DMA
    hbm, inside = pl.BlockSpec(memory_space=pltpu.HBM), pl.BlockSpec(memory_space=pltpu.VMEM)
    shape = jax.ShapeDtypeStruct
    args = [pltpu.with_memory_space_constraint(a, pltpu.HBM) for a in (
        forward_field, adjoint_start, modulus, misfit, row_owner.reshape(1, rows), row_cell.reshape(1, rows))]
    kept = pl.pallas_call(
        window,
        out_shape=(vm((C, S + 4, D, N), f32), vm((3, C, S + 4, D, N), f32), vm((4, S, D, N), f32), vm((8, 128), f32)),
        in_specs=[hbm] * 6,
        out_specs=(inside,) * 4,
        scratch_shapes=[
            vm((S + 4, D, N), f32), vm((C, S + 2, D, N), f32),
            vm((2, 2, S, N), f32), vm((C, 2, 2, S, N), f32), vm((C, 2, S, N), f32), vm((3, C, 2, 2, S, N), f32),
            vm((2, 2, S, N), f32), vm((C, 2, 2, S, N), f32), vm((C, 2, S, N), f32), vm((C, 2, 2, S, N), f32),
            vm((2, 2, 8, N), f32), vm((2, 2, C, 8, N), f32), vm((2, 2, C, 8, N), f32),
            vm((6, S + 4, D, N), f32), vm((S, D, N), f32), vm((S + 4, D, N), f32), vm((C, S, D, 128), f32), vm((3, 2, 32, 128), f32),
            vm((C, rows), f32), vm((1, rows), i32), vm((1, rows), i32),
            vm((16, 4, 128), f32), vm((16, 4, 128), f32), vm((4, 32, 128), f32), vm((8, 32, 128), f32),
            vm((2, 8, 128), f32), vm((16, 8, 128), f32), vm((8, 8, 128), f32),
            dma((8,)), dma((8, 4)), dma((8, 4)), dma((7, 4)), dma((7, 4)), dma((8,)), dma((8,)),
            dma((16,)), dma((16,)), dma((8,)), dma((8,)), dma((16,)), dma((16,)), dma((8,)), dma((8,)),
        ],
        compiler_params=pltpu.CompilerParams(collective_id=0, has_side_effects=True, vmem_limit_bytes=40 << 20),
        name="window",
    )(*args)
    return pl.pallas_call(
        finish,
        out_shape=(shape((C, S, D, N), f32), shape((S, D, N), f32)),
        in_specs=[inside] * 4,
        out_specs=(hbm, hbm),
        scratch_shapes=[vm((C, S, D, N), f32), vm((S, D, N), f32), dma((2, S // CHUNK))],
        compiler_params=pltpu.CompilerParams(vmem_limit_bytes=40 << 20),
        name="finish",
    )(*[pltpu.with_memory_space_constraint(a, pltpu.VMEM) for a in kept])


def solution(mesh):
    placed = (
        P(None, "strike", "depth", None),
        P(None, "strike", "depth", None),
        P("strike", "depth", None),
        P(None, ("strike", "depth")),
        P(("strike", "depth"), None),
        P(("strike", "depth")),
    )
    return jax.shard_map(
        on_device,
        mesh=mesh,
        in_specs=placed,
        out_specs=(P(None, "strike", "depth", None), P("strike", "depth", None)),
        check_vma=False,
    )
```
